128 devices in a mesh: path: 16 (over z, y), mp: 8 (over x, core).
Axes of the slice: x: 4, y: 4, z: 4, core: 2. Of those that a mesh axis runs over, the one named last changes fastest.
Arguments:
- features: bfloat16 [8192, 4096], P(('path', 'mp')), may hold values from -6 to 6
- targets: bfloat16 [8192, 4096], P('path', 'mp'), may hold values from -3 to 3
- module_table: bfloat16 [16, 4096, 4096], P(None, ('path', 'mp')), may hold values from -0.09375 to 0.09375
- momentum: bfloat16 [16, 4096, 4096], P(None, ('path', 'mp')), may hold values from -0.049804688 to 0.049804688
- path_lists: int32 [16, 2], replicated, may hold values from 0 to 15, all different within a row
Outputs:
- momentum_out: bfloat16 [16, 4096, 4096], P(None, ('path', 'mp'))
- evaluated: bfloat16 [8192, 4096], P('path', 'mp')
The draws below stay inside these ranges and needn't reach their ends.
Inputs may be any that keep to these rules, and one draw needn't show every extreme that they name: `path_lists`: each path names 2 different modules, and every module is named by at least one path.
All inputs are finite; a program needn't handle non-finite values.
Results may differ from the reference program's by a relative error of at most 0.0075.
The reference program's roundings to bfloat16 on the way count: a program that leaves them out, or rounds other values in their place, can miss the bound.
Values may be sent and summed in bfloat16 or wider, within the bound.
A program may use at most 128 MiB of HBM per device.

```python
import jax
import jax.numpy as jnp
from jax import lax

D = 4096
MODULES = 16
TOP = 2
INNER = 2
TOK_PATH = 512
TOKENS = 8192
N_PATH = 16


def block_levels(stream_key, shape, shards, smallest, high):
    gain, own = 1.0, jax.random.fold_in(stream_key, 6)
    for axis_at, blocks in shards:
        steps = jnp.exp(jax.random.uniform(jax.random.fold_in(own, axis_at), (blocks,), jnp.float32, smallest / len(shards), high / len(shards)))
        gain = gain * jnp.repeat(steps, shape[axis_at] // blocks).reshape([-1 if axis == axis_at else 1 for axis in range(len(shape))])
    return gain


def different_ones(stream_key, rows, amount, top, lift):
    order = jax.random.permutation(jax.random.fold_in(stream_key, 1), amount)
    pull = order
    for power in range(3):
        pull = pull * pull // amount
    pull = pull * lift // amount
    tickets = jax.random.randint(jax.random.fold_in(stream_key, 2), (rows, amount), 0, 4096) + pull
    sure = jax.random.permutation(jax.random.fold_in(stream_key, 3), rows)[jnp.arange(amount) % rows]
    tickets = jnp.where(jnp.arange(rows)[:, None] == sure[None, :], 1 << 14, tickets)
    priority = tickets * amount + jnp.arange(amount)
    return lax.top_k(priority.astype(jnp.int32), top)[1].astype(jnp.int32)


def normal_values(stream_key, dims, spread, most, split=(), held_as=jnp.bfloat16):
    factor_of = block_levels(stream_key, dims, split, -0.22, 0.18) if split else 1.0
    entries = jax.random.normal(stream_key, dims, jnp.float32) * spread * factor_of
    return jnp.minimum(jnp.maximum(entries, -most), most).astype(held_as)


def setup_inputs(seed: int = 0) -> dict:
    key_list = jax.random.split(jax.random.key(seed), 6)
    return {
        "features": normal_values(key_list[0], (TOKENS, D), 1.0, 6.0, ((0, 128),)),
        "targets": normal_values(key_list[1], (TOKENS, D), 0.5, 3.0, ((0, 16), (1, 8))),
        "module_table": normal_values(key_list[2], (MODULES, D, D), D ** -0.5, 0.09375, ((1, 128),)),
        "momentum": normal_values(key_list[3], (MODULES, D, D), 0.008, 0.049804688, ((1, 128),)),
        "path_lists": different_ones(key_list[4], N_PATH, MODULES, TOP, 2048),
    }


beta_first = 0.9
beta_second = 0.95
adam_epsilon = 1e-05
inner_rate = 0.004
weight_decay = 0.1
outer_rate = 0.7
outer_momentum = 0.9

def normalize(features):
    values = features.astype(jnp.float32)
    factor = lax.rsqrt(lax.optimization_barrier(jnp.mean(values * values, axis=-1, keepdims=True)) + 1e-05)
    return (values * factor).astype(jnp.bfloat16)

def adam_update(master, first, second, gradient, counter):
    first = beta_first * first + (1.0 - beta_first) * gradient
    second = beta_second * second + (1.0 - beta_second) * gradient * gradient
    first_hat = first / (1.0 - beta_first ** counter)
    second_hat = second / (1.0 - beta_second ** counter)
    master = master - inner_rate * (first_hat / (jnp.sqrt(second_hat) + adam_epsilon) + weight_decay * master)
    return (master, first, second)

def path_round(normed, target, start):
    master = start.astype(jnp.float32)
    first = jnp.zeros_like(master)
    second = jnp.zeros_like(master)
    current = start
    wide = normed.astype(jnp.float32)
    goal = target.astype(jnp.float32)
    for iteration in range(1, INNER + 1):
        gate_act = jnp.dot(normed, current[0], preferred_element_type=jnp.float32)
        up_act = jnp.dot(normed, current[1], preferred_element_type=jnp.float32)
        sigma = jax.nn.sigmoid(gate_act)
        swish = gate_act * sigma
        error = (swish * up_act - goal) / TOK_PATH
        d_gate = error * up_act * sigma * (1.0 + gate_act * (1.0 - sigma))
        d_up = error * swish
        grad_gate = jnp.dot(wide.T, d_gate, precision=lax.Precision.HIGHEST, preferred_element_type=jnp.float32)
        grad_up = jnp.dot(wide.T, d_up, precision=lax.Precision.HIGHEST, preferred_element_type=jnp.float32)
        gradient = jnp.stack([grad_gate, grad_up])
        master, first, second = adam_update(master, first, second, gradient, iteration)
        current = master.astype(jnp.bfloat16)
    return (start.astype(jnp.float32) - master).astype(jnp.bfloat16)

def reference(features, targets, module_table, momentum, path_lists):
    normed = normalize(features).reshape(N_PATH, TOK_PATH, D)
    target_rows = targets.reshape(N_PATH, TOK_PATH, D)
    flat_lists = path_lists.reshape(-1).astype(jnp.int32)

    def one_path(index):
        starts = jnp.take(module_table, path_lists[index], axis=0)
        return path_round(normed[index], target_rows[index], starts)
    deltas = lax.map(one_path, jnp.arange(N_PATH, dtype=jnp.int32))
    deltas = deltas.reshape(TOP * N_PATH, D, D)
    sums = jnp.zeros((MODULES, D, D), jnp.float32)
    for slot in range(TOP * N_PATH):
        sums = sums.at[flat_lists[slot]].add(deltas[slot].astype(jnp.float32))
    select = (flat_lists[None, :] == jnp.arange(MODULES, dtype=jnp.int32)[:, None]).astype(jnp.float32)
    counts = lax.optimization_barrier(jnp.sum(select, axis=1))
    average = sums / counts[:, None, None]
    moment = outer_momentum * momentum.astype(jnp.float32) + average
    updated = (module_table.astype(jnp.float32) - outer_rate * (average + outer_momentum * moment)).astype(jnp.bfloat16)

    def evaluate(index):
        weights = jnp.take(updated, path_lists[index], axis=0)
        gate_act = jnp.dot(normed[index], weights[0], preferred_element_type=jnp.float32)
        up_act = jnp.dot(normed[index], weights[1], preferred_element_type=jnp.float32)
        return (jax.nn.silu(gate_act) * up_act).astype(jnp.bfloat16)
    evaluated = lax.map(evaluate, jnp.arange(N_PATH, dtype=jnp.int32)).reshape(N_PATH * TOK_PATH, D)
    return (moment.astype(jnp.bfloat16), evaluated)
```

```python
import functools

import jax
import jax.numpy as jnp
from jax import lax
from jax.experimental import pallas as pl
from jax.experimental.pallas import tpu as pltpu
from jax.sharding import PartitionSpec as P

TOK_PATH = 512
beta_first = 0.9
beta_second = 0.95
adam_epsilon = 1e-05
inner_rate = 0.004
weight_decay = 0.1
outer_rate = 0.7
outer_momentum = 0.9
VMEM_LIMIT = 56 * 1024 * 1024

NT = (((1,), (1,)), ((), ()))


def normalize(features):
    values = features.astype(jnp.float32)
    factor = lax.rsqrt(jnp.mean(values * values, axis=-1, keepdims=True) + 1e-05)
    return (values * factor).astype(jnp.bfloat16)


def spread_kernel(table_ref, out_ref):
    for g in range(4):
        turned = table_ref[g].T
        out_ref[:, 0, g] = turned.reshape(out_ref.shape[0], out_ref.shape[3], 128)


def spread(table, paths, shards):
    modules, rows, width = table.shape
    groups = modules * rows // 128
    wide = width // shards
    cols = wide // paths
    return pl.pallas_call(
        spread_kernel,
        grid=(shards,),
        in_specs=[pl.BlockSpec((groups, 128, wide), lambda i: (0, 0, i))],
        out_specs=pl.BlockSpec((paths, 1, groups, cols, 128), lambda i: (0, i, 0, 0, 0)),
        out_shape=jax.ShapeDtypeStruct((paths, shards, groups, cols, 128), table.dtype),
        compiler_params=pltpu.CompilerParams(vmem_limit_bytes=VMEM_LIMIT),
        name="spread",
    )(table.reshape(groups, 128, width))


def unspread_kernel(blocks_ref, out_ref):
    for g in range(4):
        out_ref[g] = blocks_ref[:, 0, g].reshape(-1, 128).T


def unspread(blocks, modules, rows):
    paths, shards, groups, cols, _ = blocks.shape
    wide = paths * cols
    out = pl.pallas_call(
        unspread_kernel,
        grid=(shards,),
        in_specs=[pl.BlockSpec((paths, 1, groups, cols, 128), lambda i: (0, i, 0, 0, 0))],
        out_specs=pl.BlockSpec((groups, 128, wide), lambda i: (0, 0, i)),
        out_shape=jax.ShapeDtypeStruct((groups, 128, wide * shards), blocks.dtype),
        compiler_params=pltpu.CompilerParams(vmem_limit_bytes=VMEM_LIMIT),
        name="unspread",
    )(blocks)
    return out.reshape(modules, rows, wide * shards)


def swap_matrix():
    index = jnp.arange(512)
    source, module, row = index // 128, (index // 32) % 4, index % 32
    return (index[:, None] == (module * 128 + source * 32 + row)[None, :]).astype(jnp.bfloat16)


def gather_kernel(blocks_ref, swap_ref, out_ref):
    quads, cols = blocks_ref.shape[0] // 4, blocks_ref.shape[2]
    for k in range(quads):
        line = jnp.concatenate([blocks_ref[4 * k + s, 0] for s in range(4)], axis=1)
        turned = jnp.dot(line, swap_ref[...], preferred_element_type=jnp.float32).astype(jnp.bfloat16)
        for q in range(4):
            out_ref[q, :, k * 128 : (k + 1) * 128] = turned[:, q * 128 : (q + 1) * 128]


def gather_columns(blocks):
    devices, groups, cols, _ = blocks.shape
    return pl.pallas_call(
        gather_kernel,
        grid=(groups,),
        in_specs=[
            pl.BlockSpec((devices, 1, cols, 128), lambda g: (0, g, 0, 0)),
            pl.BlockSpec((512, 512), lambda g: (0, 0)),
        ],
        out_specs=pl.BlockSpec((4, cols, devices * 32), lambda g: (g, 0, 0)),
        out_shape=jax.ShapeDtypeStruct((groups * 4, cols, devices * 32), blocks.dtype),
        compiler_params=pltpu.CompilerParams(vmem_limit_bytes=VMEM_LIMIT),
        name="gather_columns",
    )(blocks, swap_matrix())


def scatter_kernel(table_ref, swap_ref, out_ref):
    quads = out_ref.shape[0] // 4
    for k in range(quads):
        line = jnp.concatenate([table_ref[q, :, k * 128 : (k + 1) * 128] for q in range(4)], axis=1)
        turned = jnp.dot(line, swap_ref[...], preferred_element_type=jnp.float32).astype(jnp.bfloat16)
        for s in range(4):
            out_ref[4 * k + s, 0] = turned[:, s * 128 : (s + 1) * 128]


def scatter_columns(table):
    modules, cols, width = table.shape
    groups, devices = modules // 4, width // 32
    return pl.pallas_call(
        scatter_kernel,
        grid=(groups,),
        in_specs=[
            pl.BlockSpec((4, cols, width), lambda g: (g, 0, 0)),
            pl.BlockSpec((512, 512), lambda g: (0, 0)),
        ],
        out_specs=pl.BlockSpec((devices, 1, cols, 128), lambda g: (0, g, 0, 0)),
        out_shape=jax.ShapeDtypeStruct((devices, groups, cols, 128), table.dtype),
        compiler_params=pltpu.CompilerParams(vmem_limit_bytes=VMEM_LIMIT),
        name="scatter_columns",
    )(table, swap_matrix())


def pieces(value):
    high = value.astype(jnp.bfloat16)
    rest = value - high.astype(jnp.float32)
    middle = rest.astype(jnp.bfloat16)
    low = (rest - middle.astype(jnp.float32)).astype(jnp.bfloat16)
    return jnp.concatenate([high, middle, low], axis=0)


def slopes(weights, normed, goal):
    cols = goal.shape[0]
    both = lax.dot_general(weights, normed, NT, preferred_element_type=jnp.float32)
    gate_act, up_act = both[:cols], both[cols:]
    sigma = jax.nn.sigmoid(gate_act)
    swish = gate_act * sigma
    error = (swish * up_act - goal) / TOK_PATH
    d_gate = error * up_act * sigma * (1.0 + gate_act * (1.0 - sigma))
    d_up = error * swish
    return pieces(jnp.concatenate([d_gate, d_up], axis=0))


TILE = 512


def inner_kernel(lists_ref, normed_ref, goal_ref, table_ref, sums_ref, start, current, first_grad, slope):
    path = pl.program_id(0)
    gate, up = lists_ref[2 * path], lists_ref[2 * path + 1]
    cols = goal_ref.shape[1]
    width = normed_ref.shape[1]

    @pl.when(path == 0)
    def _():
        sums_ref[...] = jnp.zeros_like(sums_ref)

    start[:cols] = table_ref[gate]
    start[cols:] = table_ref[up]
    goal = goal_ref[0].astype(jnp.float32)
    slope[...] = slopes(start[...], normed_ref[...], goal)

    def product(columns):
        parts = jnp.dot(slope[...], normed_ref[:, columns], preferred_element_type=jnp.float32)
        return parts[: 2 * cols] + (parts[2 * cols : 4 * cols] + parts[4 * cols :])

    def after_first(begin, grad):
        return begin - inner_rate * (grad / (jnp.abs(grad) + adam_epsilon) + weight_decay * begin)

    for j in range(width // TILE):
        columns = slice(j * TILE, (j + 1) * TILE)
        grad = product(columns)
        first_grad[:, columns] = grad
        begin = start[:, columns].astype(jnp.float32)
        current[:, columns] = after_first(begin, grad).astype(jnp.bfloat16)

    slope[...] = slopes(current[...], normed_ref[...], goal)
    for j in range(width // TILE):
        columns = slice(j * TILE, (j + 1) * TILE)
        grad = product(columns)
        before = first_grad[:, columns]
        begin = start[:, columns].astype(jnp.float32)
        master = after_first(begin, before)
        first = (beta_first * (1.0 - beta_first) / (1.0 - beta_first**2)) * before + (
            (1.0 - beta_first) / (1.0 - beta_first**2)
        ) * grad
        second = (beta_second * (1.0 - beta_second) / (1.0 - beta_second**2)) * before * before + (
            (1.0 - beta_second) / (1.0 - beta_second**2)
        ) * grad * grad
        master = master - inner_rate * (
            first / (jnp.sqrt(second) + adam_epsilon) + weight_decay * master
        )
        delta = (begin - master).astype(jnp.bfloat16).astype(jnp.float32)
        sums_ref[gate, :, columns] += delta[:cols]
        sums_ref[up, :, columns] += delta[cols:]


def inner_steps(lists, normed, goals, table):
    modules, cols, width = table.shape
    paths = goals.shape[0]
    tokens = normed.shape[0]
    return pl.pallas_call(
        inner_kernel,
        grid_spec=pltpu.PrefetchScalarGridSpec(
            num_scalar_prefetch=1,
            grid=(paths,),
            in_specs=[
                pl.BlockSpec((TOK_PATH, width), lambda p, s: (p, 0)),
                pl.BlockSpec((1, cols, TOK_PATH), lambda p, s: (p, 0, 0)),
                pl.BlockSpec((modules, cols, width), lambda p, s: (0, 0, 0)),
            ],
            out_specs=pl.BlockSpec((modules, cols, width), lambda p, s: (0, 0, 0)),
            scratch_shapes=[
                pltpu.VMEM((2 * cols, width), jnp.bfloat16),
                pltpu.VMEM((2 * cols, width), jnp.bfloat16),
                pltpu.VMEM((2 * cols, width), jnp.float32),
                pltpu.VMEM((6 * cols, TOK_PATH), jnp.bfloat16),
            ],
        ),
        out_shape=jax.ShapeDtypeStruct((modules, cols, width), jnp.float32),
        compiler_params=pltpu.CompilerParams(vmem_limit_bytes=VMEM_LIMIT),
        cost_estimate=pl.CostEstimate(
            flops=32 * tokens * width * cols, bytes_accessed=2 * tokens * width, transcendentals=0
        ),
        name="inner_steps",
    )(lists, normed, goals, table)


def evaluate_kernel(lists_ref, normed_ref, table_ref, out_ref, weights):
    path = pl.program_id(0)
    cols = out_ref.shape[1]
    weights[:cols] = table_ref[lists_ref[2 * path]]
    weights[cols:] = table_ref[lists_ref[2 * path + 1]]
    both = lax.dot_general(weights[...], normed_ref[...], NT, preferred_element_type=jnp.float32)
    gate_act = both[:cols]
    out_ref[0] = (gate_act * jax.nn.sigmoid(gate_act) * both[cols:]).astype(jnp.bfloat16)


def evaluate(lists, normed, table):
    modules, cols, width = table.shape
    tokens = normed.shape[0]
    paths = tokens // TOK_PATH
    return pl.pallas_call(
        evaluate_kernel,
        grid_spec=pltpu.PrefetchScalarGridSpec(
            num_scalar_prefetch=1,
            grid=(paths,),
            in_specs=[
                pl.BlockSpec((TOK_PATH, width), lambda p, s: (p, 0)),
                pl.BlockSpec((modules, cols, width), lambda p, s: (0, 0, 0)),
            ],
            out_specs=pl.BlockSpec((1, cols, TOK_PATH), lambda p, s: (p, 0, 0)),
            scratch_shapes=[pltpu.VMEM((2 * cols, width), jnp.bfloat16)],
        ),
        out_shape=jax.ShapeDtypeStruct((paths, cols, TOK_PATH), jnp.bfloat16),
        compiler_params=pltpu.CompilerParams(vmem_limit_bytes=VMEM_LIMIT),
        cost_estimate=pl.CostEstimate(
            flops=4 * tokens * width * cols, bytes_accessed=2 * tokens * width, transcendentals=0
        ),
        name="evaluate",
    )(lists, normed, table)


def exchange(blocks, axes):
    return lax.all_to_all(blocks, axes, split_axis=0, concat_axis=0, tiled=True)


def local(features, targets, module_table, momentum, path_lists):
    paths = lax.axis_size("path")
    shards = lax.axis_size("mp")
    modules, rows_own, width = module_table.shape
    cols = width // (paths * shards)
    lists = path_lists.reshape(-1)
    both = ("path", "mp")

    def to_columns(table):
        blocks = spread(table, paths, shards)
        blocks = blocks.reshape((paths * shards,) + blocks.shape[2:])
        return gather_columns(exchange(blocks, both))

    def to_rows(table):
        blocks = exchange(scatter_columns(table), both)
        return unspread(blocks.reshape((paths, shards) + blocks.shape[1:]), modules, rows_own)

    normed = lax.all_gather(normalize(features), both, axis=0, tiled=True)
    table = to_columns(module_table)
    goals = exchange(targets.T.reshape(paths, cols, TOK_PATH), "path")
    speed = to_columns(momentum)
    sums = inner_steps(lists, normed, goals, table)
    select = lists[None, :] == jnp.arange(modules, dtype=jnp.int32)[:, None]
    counts = jnp.sum(select.astype(jnp.float32), axis=1)
    average = sums / counts[:, None, None]
    moment = outer_momentum * speed.astype(jnp.float32) + average
    updated = (
        table.astype(jnp.float32) - outer_rate * (average + outer_momentum * moment)
    ).astype(jnp.bfloat16)
    momentum_out = to_rows(moment.astype(jnp.bfloat16))
    evaluated = evaluate(lists, normed, updated)
    evaluated = exchange(evaluated, "path").reshape(paths * cols, TOK_PATH).T
    return (momentum_out, evaluated)


def solution(mesh):
    return jax.shard_map(
        local,
        mesh=mesh,
        in_specs=(
            P(("path", "mp"), None),
            P("path", "mp"),
            P(None, ("path", "mp"), None),
            P(None, ("path", "mp"), None),
            P(),
        ),
        out_specs=(P(None, ("path", "mp"), None), P("path", "mp")),
        check_vma=False,
    )
```

```python
import functools

import jax
import jax.numpy as jnp
from jax import lax
from jax.experimental import pallas as pl
from jax.experimental.pallas import tpu as pltpu
from jax.sharding import PartitionSpec as P

TOK_PATH = 512
beta_first = 0.9
beta_second = 0.95
adam_epsilon = 1e-05
inner_rate = 0.004
weight_decay = 0.1
outer_rate = 0.7
outer_momentum = 0.9
VMEM_LIMIT = 56 * 1024 * 1024

NT = (((1,), (1,)), ((), ()))


def normalize(features):
    values = features.astype(jnp.float32)
    factor = lax.rsqrt(jnp.mean(values * values, axis=-1, keepdims=True) + 1e-05)
    return (values * factor).astype(jnp.bfloat16)


RING = 4
PARTS = (("x", "y", "z", 0, 1408), ("y", "z", "x", 1408, 2816), ("z", "x", "y", 2816, 4096))
ARRIVALS = 9


def gather_tokens_kernel(own_ref, out_ref, local_sem, send_sem, recv_sem):
    path, shard = lax.axis_index("path"), lax.axis_index("mp")
    me = {"z": path // RING, "y": path % RING, "x": shard // 2}
    core = shard % 2

    def shifted(axis, step):
        return {**me, axis: (me[axis] + (step + RING)) % RING}

    def device(at, which):
        return (at["z"] * RING + at["y"], at["x"] * 2 + which)

    everyone = [device(shifted(axis, step), core) for axis in "xyz" for step in (1, -1)]
    everyone.append(device(me, 1 - core))
    barrier = pltpu.get_barrier_semaphore()
    for other in everyone:
        pl.semaphore_signal(barrier, inc=1, device_id=other, device_id_type=pl.DeviceIdType.MESH)
    pl.semaphore_wait(barrier, len(everyone))

    whole = pl.ds(0, RING)
    rows = own_ref.shape[0]
    counter = [0]
    sends = []

    def view(at, which, lines, columns):
        return out_ref.at[at["z"], at["y"], at["x"], which, lines, columns]

    def send(at, target, lines, columns, source=None):
        number = counter[0]
        counter[0] += 1
        block = view(at, core, lines, columns)
        copy = pltpu.make_async_remote_copy(
            src_ref=block if source is None else source,
            dst_ref=block,
            send_sem=send_sem.at[number],
            recv_sem=recv_sem.at[number],
            device_id=target,
            device_id_type=pl.DeviceIdType.MESH,
        )
        copy.start()
        sends.append(copy)
        return number

    def arrived(number, at, lines, columns, which=core):
        block = view(at, which, lines, columns)
        pltpu.make_async_remote_copy(
            src_ref=block,
            dst_ref=block,
            send_sem=send_sem.at[number],
            recv_sem=recv_sem.at[number],
            device_id=device(me, 1 - core),
            device_id_type=pl.DeviceIdType.MESH,
        ).wait_recv()

    full, low, high = pl.ds(0, rows), pl.ds(0, rows // 2), pl.ds(rows // 2, rows // 2)
    sibling = device(me, 1 - core)
    sibling_arrivals = []

    def share(at, columns):
        number = send(at, sibling, full, columns)
        sibling_arrivals.append((number, at, columns))

    own_copy = pltpu.make_async_copy(own_ref, view(me, core, full, pl.ds(0, own_ref.shape[1])), local_sem)
    own_copy.start()

    first = {}
    for part, (a, b, c, begin, end) in enumerate(PARTS):
        columns = pl.ds(begin, end - begin)
        source = own_ref.at[:, columns]
        first[part] = [
            send(me, device(shifted(a, step), core), full, columns, source) for step in (1, -1)
        ]
    own_copy.wait()

    second = {part: [] for part in range(len(PARTS))}

    def send_both(at, axis, columns):
        return [send(at, device(shifted(axis, step), core), full, columns) for step in (1, -1)]

    for part, (a, b, c, begin, end) in enumerate(PARTS):
        second[part].append(send_both(me, b, pl.ds(begin, end - begin)))
    halves = {}
    for index, step in ((0, 1), (1, -1)):
        for part, (a, b, c, begin, end) in enumerate(PARTS):
            columns = pl.ds(begin, end - begin)
            origin = shifted(a, -step)
            arrived(first[part][index], origin, full, columns)
            lines = low if index == 0 else high
            halves[part, index] = send(origin, device(shifted(a, step), core), lines, columns)
            second[part].append(send_both(origin, b, columns))
    for part, (a, b, c, begin, end) in enumerate(PARTS):
        columns = pl.ds(begin, end - begin)
        origin = shifted(a, 2)
        arrived(halves[part, 0], origin, low, columns)
        arrived(halves[part, 1], origin, high, columns)
        second[part].append(send_both(origin, b, columns))

    third = {part: [] for part in range(len(PARTS))}
    for part, (a, b, c, begin, end) in enumerate(PARTS):
        columns = pl.ds(begin, end - begin)
        line = {**me, a: whole}
        third[part].append(send_both(line, c, columns))
        share(line, columns)

    def origins(a):
        return [me[a], (me[a] + 3) % RING, (me[a] + 1) % RING, (me[a] + 2) % RING]

    for index, step in ((0, 1), (1, -1)):
        lines = low if index == 0 else high
        for part, (a, b, c, begin, end) in enumerate(PARTS):
            columns = pl.ds(begin, end - begin)
            far = shifted(b, -step)
            for unit, place in enumerate(origins(a)):
                origin = {**far, a: place}
                arrived(second[part][unit][index], origin, full, columns)
                halves[part, index, unit] = send(origin, device(shifted(b, step), core), lines, columns)
            line = {**far, a: whole}
            third[part].append(send_both(line, c, columns))
            share(line, columns)
    for part, (a, b, c, begin, end) in enumerate(PARTS):
        columns = pl.ds(begin, end - begin)
        far = shifted(b, 2)
        for unit, place in enumerate(origins(a)):
            origin = {**far, a: place}
            arrived(halves[part, 0, unit], origin, low, columns)
            arrived(halves[part, 1, unit], origin, high, columns)
        line = {**far, a: whole}
        third[part].append(send_both(line, c, columns))
        share(line, columns)

    for unit in range(RING):
        for index, step in ((0, 1), (1, -1)):
            lines = low if index == 0 else high
            for part, (a, b, c, begin, end) in enumerate(PARTS):
                columns = pl.ds(begin, end - begin)
                far = {**shifted(c, -step), a: whole, b: origins(b)[unit]}
                arrived(third[part][unit][index], far, full, columns)
                halves[part, "last", index, unit] = send(far, device(shifted(c, step), core), lines, columns)
                share(far, columns)
    for unit in range(RING):
        for part, (a, b, c, begin, end) in enumerate(PARTS):
            columns = pl.ds(begin, end - begin)
            far = {**shifted(c, 2), a: whole, b: origins(b)[unit]}
            arrived(halves[part, "last", 0, unit], far, low, columns)
            arrived(halves[part, "last", 1, unit], far, high, columns)
            share(far, columns)
    for number, at, columns in sibling_arrivals:
        arrived(number, at, full, columns, 1 - core)
    for copy in sends:
        copy.wait_send()


COPIES = 156


def gather_tokens(own):
    rows, width = own.shape
    paths, shards = lax.axis_size("path"), lax.axis_size("mp")
    out = pl.pallas_call(
        gather_tokens_kernel,
        in_specs=[pl.BlockSpec(memory_space=pl.ANY)],
        out_specs=pl.BlockSpec(memory_space=pl.ANY),
        out_shape=jax.ShapeDtypeStruct((paths // RING, RING, shards // 2, 2, rows, width), own.dtype),
        scratch_shapes=[
            pltpu.SemaphoreType.DMA,
            pltpu.SemaphoreType.DMA((COPIES,)),
            pltpu.SemaphoreType.DMA((COPIES,)),
        ],
        compiler_params=pltpu.CompilerParams(collective_id=0, has_side_effects=True),
        cost_estimate=pl.CostEstimate(flops=0, bytes_accessed=4 * paths * shards * rows * width, transcendentals=0),
        name="gather_tokens",
    )(own)
    return out.reshape(paths * shards * rows, width)


def spread_kernel(table_ref, out_ref):
    for g in range(4):
        turned = table_ref[g].T
        out_ref[:, 0, g] = turned.reshape(out_ref.shape[0], out_ref.shape[3], 128)


def spread(table, paths, shards):
    modules, rows, width = table.shape
    groups = modules * rows // 128
    wide = width // shards
    cols = wide // paths
    return pl.pallas_call(
        spread_kernel,
        grid=(shards,),
        in_specs=[pl.BlockSpec((groups, 128, wide), lambda i: (0, 0, i))],
        out_specs=pl.BlockSpec((paths, 1, groups, cols, 128), lambda i: (0, i, 0, 0, 0)),
        out_shape=jax.ShapeDtypeStruct((paths, shards, groups, cols, 128), table.dtype),
        compiler_params=pltpu.CompilerParams(vmem_limit_bytes=VMEM_LIMIT),
        name="spread",
    )(table.reshape(groups, 128, width))


def unspread_kernel(blocks_ref, out_ref):
    for g in range(4):
        out_ref[g] = blocks_ref[:, 0, g].reshape(-1, 128).T


def unspread(blocks, modules, rows):
    paths, shards, groups, cols, _ = blocks.shape
    wide = paths * cols
    out = pl.pallas_call(
        unspread_kernel,
        grid=(shards,),
        in_specs=[pl.BlockSpec((paths, 1, groups, cols, 128), lambda i: (0, i, 0, 0, 0))],
        out_specs=pl.BlockSpec((groups, 128, wide), lambda i: (0, 0, i)),
        out_shape=jax.ShapeDtypeStruct((groups, 128, wide * shards), blocks.dtype),
        compiler_params=pltpu.CompilerParams(vmem_limit_bytes=VMEM_LIMIT),
        name="unspread",
    )(blocks)
    return out.reshape(modules, rows, wide * shards)


def swap_matrix():
    index = jnp.arange(512)
    source, module, row = index // 128, (index // 32) % 4, index % 32
    return (index[:, None] == (module * 128 + source * 32 + row)[None, :]).astype(jnp.bfloat16)


def gather_kernel(blocks_ref, swap_ref, out_ref):
    quads, cols = blocks_ref.shape[0] // 4, blocks_ref.shape[2]
    blocks = blocks_ref[:, 0].reshape(quads, 4, cols, 128)
    line = jnp.concatenate([blocks[:, s].reshape(quads * cols, 128) for s in range(4)], axis=1)
    turned = jnp.dot(line, swap_ref[...], preferred_element_type=jnp.float32).astype(jnp.bfloat16)
    turned = turned.reshape(quads, cols, 512)
    for k in range(quads):
        for q in range(4):
            out_ref[q, :, k * 128 : (k + 1) * 128] = turned[k, :, q * 128 : (q + 1) * 128]


def gather_columns(blocks):
    devices, groups, cols, _ = blocks.shape
    return pl.pallas_call(
        gather_kernel,
        grid=(groups,),
        in_specs=[
            pl.BlockSpec((devices, 1, cols, 128), lambda g: (0, g, 0, 0)),
            pl.BlockSpec((512, 512), lambda g: (0, 0)),
        ],
        out_specs=pl.BlockSpec((4, cols, devices * 32), lambda g: (g, 0, 0)),
        out_shape=jax.ShapeDtypeStruct((groups * 4, cols, devices * 32), blocks.dtype),
        compiler_params=pltpu.CompilerParams(vmem_limit_bytes=VMEM_LIMIT),
        name="gather_columns",
    )(blocks, swap_matrix())


CHUNK = 8


def outer_kernel(counts_ref, sums_ref, table_ref, speed_ref, swap_ref, updated_ref, out_ref):
    group = pl.program_id(0)
    quads, cols = out_ref.shape[0] // 4, out_ref.shape[2]
    counts = [counts_ref[4 * group + q] for q in range(4)]
    for begin in range(0, quads, CHUNK):
        blocks = speed_ref[4 * begin : 4 * (begin + CHUNK), 0].reshape(CHUNK, 4, cols, 128)
        line = jnp.concatenate([blocks[:, s].reshape(CHUNK * cols, 128) for s in range(4)], axis=1)
        speed = jnp.dot(line, swap_ref[...], preferred_element_type=jnp.float32).reshape(CHUNK, cols, 512)
        lines = []
        for k in range(CHUNK):
            pieces_of = []
            for q in range(4):
                columns = slice((begin + k) * 128, (begin + k + 1) * 128)
                average = sums_ref[q, :, columns] / counts[q]
                moment = outer_momentum * speed[k, :, q * 128 : (q + 1) * 128] + average
                begun = table_ref[q, :, columns].astype(jnp.float32)
                updated_ref[q, :, columns] = (
                    begun - outer_rate * (average + outer_momentum * moment)
                ).astype(jnp.bfloat16)
                pieces_of.append(moment.astype(jnp.bfloat16))
            lines.append(jnp.concatenate(pieces_of, axis=1))
        line = jnp.concatenate(lines, axis=0)
        turned = jnp.dot(line, swap_ref[...], preferred_element_type=jnp.float32).astype(jnp.bfloat16)
        turned = turned.reshape(CHUNK, cols, 512)
        for k in range(CHUNK):
            for s in range(4):
                out_ref[4 * (begin + k) + s, 0] = turned[k, :, s * 128 : (s + 1) * 128]


def outer_step(counts, sums, table, speed):
    modules, cols, width = table.shape
    devices, groups = speed.shape[:2]
    rows = pl.BlockSpec((4, cols, width), lambda g: (g, 0, 0))
    blocks = pl.BlockSpec((devices, 1, cols, 128), lambda g: (0, g, 0, 0))
    return pl.pallas_call(
        outer_kernel,
        grid=(groups,),
        in_specs=[
            pl.BlockSpec(memory_space=pltpu.SMEM),
            rows,
            rows,
            blocks,
            pl.BlockSpec((512, 512), lambda g: (0, 0)),
        ],
        out_specs=[rows, blocks],
        out_shape=[
            jax.ShapeDtypeStruct(table.shape, table.dtype),
            jax.ShapeDtypeStruct(speed.shape, speed.dtype),
        ],
        compiler_params=pltpu.CompilerParams(vmem_limit_bytes=VMEM_LIMIT),
        name="outer_step",
    )(counts, sums, table, speed, swap_matrix())


def pieces(value):
    high = value.astype(jnp.bfloat16)
    rest = value - high.astype(jnp.float32)
    middle = rest.astype(jnp.bfloat16)
    low = (rest - middle.astype(jnp.float32)).astype(jnp.bfloat16)
    return jnp.concatenate([high, middle, low], axis=0)


def slopes(weights, normed, goal):
    cols = goal.shape[0]
    both = jnp.dot(weights, normed, preferred_element_type=jnp.float32)
    gate_act, up_act = both[:cols], both[cols:]
    sigma = jax.nn.sigmoid(gate_act)
    swish = gate_act * sigma
    error = (swish * up_act - goal) / TOK_PATH
    d_gate = error * up_act * sigma * (1.0 + gate_act * (1.0 - sigma))
    d_up = error * swish
    return pieces(jnp.concatenate([d_gate, d_up], axis=0))


TILE = 512


def inner_kernel(lists_ref, normed_ref, goal_ref, table_ref, sums_ref, start, current, first_grad, slope, turned):
    path = pl.program_id(0)
    gate, up = lists_ref[2 * path], lists_ref[2 * path + 1]
    cols = goal_ref.shape[1]
    width = normed_ref.shape[1]

    @pl.when(path == 0)
    def _():
        sums_ref[...] = jnp.zeros_like(sums_ref)

    start[:cols] = table_ref[gate]
    start[cols:] = table_ref[up]
    goal = goal_ref[0].astype(jnp.float32)
    for j in range(width // TILE):
        turned[j * TILE : (j + 1) * TILE, :] = normed_ref[:, j * TILE : (j + 1) * TILE].T
    slope[...] = slopes(start[...], turned[...], goal)

    def product(columns):
        parts = jnp.dot(slope[...], normed_ref[:, columns], preferred_element_type=jnp.float32)
        return parts[: 2 * cols] + (parts[2 * cols : 4 * cols] + parts[4 * cols :])

    def after_first(begin, grad):
        return begin - inner_rate * (grad / (jnp.abs(grad) + adam_epsilon) + weight_decay * begin)

    for j in range(width // TILE):
        columns = slice(j * TILE, (j + 1) * TILE)
        grad = product(columns)
        first_grad[:, columns] = grad
        begin = start[:, columns].astype(jnp.float32)
        current[:, columns] = after_first(begin, grad).astype(jnp.bfloat16)

    slope[...] = slopes(current[...], turned[...], goal)
    for j in range(width // TILE):
        columns = slice(j * TILE, (j + 1) * TILE)
        grad = product(columns)
        before = first_grad[:, columns]
        begin = start[:, columns].astype(jnp.float32)
        master = after_first(begin, before)
        first = (beta_first * (1.0 - beta_first) / (1.0 - beta_first**2)) * before + (
            (1.0 - beta_first) / (1.0 - beta_first**2)
        ) * grad
        second = (beta_second * (1.0 - beta_second) / (1.0 - beta_second**2)) * before * before + (
            (1.0 - beta_second) / (1.0 - beta_second**2)
        ) * grad * grad
        master = master - inner_rate * (
            first / (jnp.sqrt(second) + adam_epsilon) + weight_decay * master
        )
        delta = (begin - master).astype(jnp.bfloat16).astype(jnp.float32)
        sums_ref[gate, :, columns] += delta[:cols]
        sums_ref[up, :, columns] += delta[cols:]


def inner_steps(lists, normed, goals, table):
    modules, cols, width = table.shape
    paths = goals.shape[0]
    tokens = normed.shape[0]
    return pl.pallas_call(
        inner_kernel,
        grid_spec=pltpu.PrefetchScalarGridSpec(
            num_scalar_prefetch=1,
            grid=(paths,),
            in_specs=[
                pl.BlockSpec((TOK_PATH, width), lambda p, s: (p, 0)),
                pl.BlockSpec((1, cols, TOK_PATH), lambda p, s: (p, 0, 0)),
                pl.BlockSpec((modules, cols, width), lambda p, s: (0, 0, 0)),
            ],
            out_specs=pl.BlockSpec((modules, cols, width), lambda p, s: (0, 0, 0)),
            scratch_shapes=[
                pltpu.VMEM((2 * cols, width), jnp.bfloat16),
                pltpu.VMEM((2 * cols, width), jnp.bfloat16),
                pltpu.VMEM((2 * cols, width), jnp.float32),
                pltpu.VMEM((6 * cols, TOK_PATH), jnp.bfloat16),
                pltpu.VMEM((width, TOK_PATH), jnp.bfloat16),
            ],
        ),
        out_shape=jax.ShapeDtypeStruct((modules, cols, width), jnp.float32),
        compiler_params=pltpu.CompilerParams(vmem_limit_bytes=VMEM_LIMIT),
        cost_estimate=pl.CostEstimate(
            flops=32 * tokens * width * cols, bytes_accessed=2 * tokens * width, transcendentals=0
        ),
        name="inner_steps",
    )(lists, normed, goals, table)


def evaluate_kernel(lists_ref, normed_ref, table_ref, out_ref, weights):
    path = pl.program_id(0)
    cols = out_ref.shape[1]
    weights[:cols] = table_ref[lists_ref[2 * path]]
    weights[cols:] = table_ref[lists_ref[2 * path + 1]]
    both = lax.dot_general(weights[...], normed_ref[...], NT, preferred_element_type=jnp.float32)
    gate_act = both[:cols]
    out_ref[0] = (gate_act * jax.nn.sigmoid(gate_act) * both[cols:]).astype(jnp.bfloat16)


def evaluate(lists, normed, table):
    modules, cols, width = table.shape
    tokens = normed.shape[0]
    paths = tokens // TOK_PATH
    return pl.pallas_call(
        evaluate_kernel,
        grid_spec=pltpu.PrefetchScalarGridSpec(
            num_scalar_prefetch=1,
            grid=(paths,),
            in_specs=[
                pl.BlockSpec((TOK_PATH, width), lambda p, s: (p, 0)),
                pl.BlockSpec((modules, cols, width), lambda p, s: (0, 0, 0)),
            ],
            out_specs=pl.BlockSpec((1, cols, TOK_PATH), lambda p, s: (p, 0, 0)),
            scratch_shapes=[pltpu.VMEM((2 * cols, width), jnp.bfloat16)],
        ),
        out_shape=jax.ShapeDtypeStruct((paths, cols, TOK_PATH), jnp.bfloat16),
        compiler_params=pltpu.CompilerParams(vmem_limit_bytes=VMEM_LIMIT),
        cost_estimate=pl.CostEstimate(
            flops=4 * tokens * width * cols, bytes_accessed=2 * tokens * width, transcendentals=0
        ),
        name="evaluate",
    )(lists, normed, table)


def exchange(blocks, axes):
    return lax.all_to_all(blocks, axes, split_axis=0, concat_axis=0, tiled=True)


def local(features, targets, module_table, momentum, path_lists):
    paths = lax.axis_size("path")
    shards = lax.axis_size("mp")
    modules, rows_own, width = module_table.shape
    cols = width // (paths * shards)
    lists = path_lists.reshape(-1)
    both = ("path", "mp")

    def sent(table):
        blocks = spread(table, paths, shards)
        return exchange(blocks.reshape((paths * shards,) + blocks.shape[2:]), both)

    normed = gather_tokens(normalize(features))
    table = gather_columns(sent(module_table))
    goals = exchange(targets.T.reshape(paths, cols, TOK_PATH), "path")
    speed = sent(momentum)
    select = lists[None, :] == jnp.arange(modules, dtype=jnp.int32)[:, None]
    counts = jnp.sum(select.astype(jnp.float32), axis=1)
    sums = inner_steps(lists, normed, goals, table)
    updated, blocks = lax.optimization_barrier(outer_step(counts, sums, table, speed))
    blocks = exchange(blocks, both)
    momentum_out = unspread(blocks.reshape((paths, shards) + blocks.shape[1:]), modules, rows_own)
    evaluated = evaluate(lists, normed, updated)
    evaluated = exchange(evaluated, "path").reshape(paths * cols, TOK_PATH).T
    return (momentum_out, evaluated)


def solution(mesh):
    return jax.shard_map(
        local,
        mesh=mesh,
        in_specs=(
            P(("path", "mp"), None),
            P("path", "mp"),
            P(None, ("path", "mp"), None),
            P(None, ("path", "mp"), None),
            P(),
        ),
        out_specs=(P(None, ("path", "mp"), None), P("path", "mp")),
        check_vma=False,
    )
```

```python
import functools

import jax
import jax.numpy as jnp
from jax import lax
from jax.experimental import pallas as pl
from jax.experimental.pallas import tpu as pltpu
from jax.sharding import PartitionSpec as P

TOK_PATH = 512
beta_first = 0.9
beta_second = 0.95
adam_epsilon = 1e-05
inner_rate = 0.004
weight_decay = 0.1
outer_rate = 0.7
outer_momentum = 0.9
VMEM_LIMIT = 56 * 1024 * 1024

NT = (((1,), (1,)), ((), ()))


def normalize(features):
    values = features.astype(jnp.float32)
    factor = lax.rsqrt(jnp.mean(values * values, axis=-1, keepdims=True) + 1e-05)
    return (values * factor).astype(jnp.bfloat16)


RING = 4
PARTS = (("x", "y", "z", 0, 1408), ("y", "z", "x", 1408, 2816), ("z", "x", "y", 2816, 4096))
ARRIVALS = 9


def gather_tokens_kernel(own_ref, goal_ref, out_ref, goals_ref, local_sem, send_sem, recv_sem, goal_sem, goals_sem):
    path, shard = lax.axis_index("path"), lax.axis_index("mp")
    me = {"z": path // RING, "y": path % RING, "x": shard // 2}
    core = shard % 2

    def shifted(axis, step):
        return {**me, axis: (me[axis] + (step + RING)) % RING}

    def device(at, which):
        return (at["z"] * RING + at["y"], at["x"] * 2 + which)

    everyone = [device(shifted(axis, step), core) for axis in "xyz" for step in (1, -1)]
    everyone.append(device(me, 1 - core))
    paths = goal_ref.shape[0]
    peers = [((path + step) % paths, shard) for step in range(1, paths)]
    everyone += peers
    barrier = pltpu.get_barrier_semaphore()
    for other in everyone:
        pl.semaphore_signal(barrier, inc=1, device_id=other, device_id_type=pl.DeviceIdType.MESH)
    pl.semaphore_wait(barrier, len(everyone))

    whole = pl.ds(0, RING)
    rows = own_ref.shape[0]
    counter = [0]
    sends = []

    def view(at, which, lines, columns):
        return out_ref.at[at["z"], at["y"], at["x"], which, lines, columns]

    def send(at, target, lines, columns, source=None):
        number = counter[0]
        counter[0] += 1
        block = view(at, core, lines, columns)
        copy = pltpu.make_async_remote_copy(
            src_ref=block if source is None else source,
            dst_ref=block,
            send_sem=send_sem.at[number],
            recv_sem=recv_sem.at[number],
            device_id=target,
            device_id_type=pl.DeviceIdType.MESH,
        )
        copy.start()
        sends.append(copy)
        return number

    def arrived(number, at, lines, columns, which=core):
        block = view(at, which, lines, columns)
        pltpu.make_async_remote_copy(
            src_ref=block,
            dst_ref=block,
            send_sem=send_sem.at[number],
            recv_sem=recv_sem.at[number],
            device_id=device(me, 1 - core),
            device_id_type=pl.DeviceIdType.MESH,
        ).wait_recv()

    full, low, high = pl.ds(0, rows), pl.ds(0, rows // 2), pl.ds(rows // 2, rows // 2)
    sibling = device(me, 1 - core)
    sibling_arrivals = []

    def share(at, columns):
        number = send(at, sibling, full, columns)
        sibling_arrivals.append((number, at, columns))

    own_copy = pltpu.make_async_copy(own_ref, view(me, core, full, pl.ds(0, own_ref.shape[1])), local_sem)
    own_copy.start()

    first = {}
    for part, (a, b, c, begin, end) in enumerate(PARTS):
        columns = pl.ds(begin, end - begin)
        source = own_ref.at[:, columns]
        first[part] = [
            send(me, device(shifted(a, step), core), full, columns, source) for step in (1, -1)
        ]
    own_copy.wait()

    own_goal = pltpu.make_async_copy(goal_ref.at[path], goals_ref.at[path], goals_sem.at[0])
    own_goal.start()
    goal_copies = []
    for step, other in enumerate(peers, 1):
        copy = pltpu.make_async_remote_copy(
            src_ref=goal_ref.at[other[0]],
            dst_ref=goals_ref.at[path],
            send_sem=goal_sem.at[step],
            recv_sem=goals_sem.at[step],
            device_id=other,
            device_id_type=pl.DeviceIdType.MESH,
        )
        copy.start()
        goal_copies.append(copy)

    second = {part: [] for part in range(len(PARTS))}

    def send_both(at, axis, columns):
        return [send(at, device(shifted(axis, step), core), full, columns) for step in (1, -1)]

    for part, (a, b, c, begin, end) in enumerate(PARTS):
        second[part].append(send_both(me, b, pl.ds(begin, end - begin)))
    halves = {}
    for index, step in ((0, 1), (1, -1)):
        for part, (a, b, c, begin, end) in enumerate(PARTS):
            columns = pl.ds(begin, end - begin)
            origin = shifted(a, -step)
            arrived(first[part][index], origin, full, columns)
            lines = low if index == 0 else high
            halves[part, index] = send(origin, device(shifted(a, step), core), lines, columns)
            second[part].append(send_both(origin, b, columns))
    for part, (a, b, c, begin, end) in enumerate(PARTS):
        columns = pl.ds(begin, end - begin)
        origin = shifted(a, 2)
        arrived(halves[part, 0], origin, low, columns)
        arrived(halves[part, 1], origin, high, columns)
        second[part].append(send_both(origin, b, columns))

    third = {part: [] for part in range(len(PARTS))}
    for part, (a, b, c, begin, end) in enumerate(PARTS):
        columns = pl.ds(begin, end - begin)
        line = {**me, a: whole}
        third[part].append(send_both(line, c, columns))
        share(line, columns)

    def origins(a):
        return [me[a], (me[a] + 3) % RING, (me[a] + 1) % RING, (me[a] + 2) % RING]

    for index, step in ((0, 1), (1, -1)):
        lines = low if index == 0 else high
        for part, (a, b, c, begin, end) in enumerate(PARTS):
            columns = pl.ds(begin, end - begin)
            far = shifted(b, -step)
            for unit, place in enumerate(origins(a)):
                origin = {**far, a: place}
                arrived(second[part][unit][index], origin, full, columns)
                halves[part, index, unit] = send(origin, device(shifted(b, step), core), lines, columns)
            line = {**far, a: whole}
            third[part].append(send_both(line, c, columns))
            share(line, columns)
    for part, (a, b, c, begin, end) in enumerate(PARTS):
        columns = pl.ds(begin, end - begin)
        far = shifted(b, 2)
        for unit, place in enumerate(origins(a)):
            origin = {**far, a: place}
            arrived(halves[part, 0, unit], origin, low, columns)
            arrived(halves[part, 1, unit], origin, high, columns)
        line = {**far, a: whole}
        third[part].append(send_both(line, c, columns))
        share(line, columns)

    for unit in range(RING):
        for index, step in ((0, 1), (1, -1)):
            lines = low if index == 0 else high
            for part, (a, b, c, begin, end) in enumerate(PARTS):
                columns = pl.ds(begin, end - begin)
                far = {**shifted(c, -step), a: whole, b: origins(b)[unit]}
                arrived(third[part][unit][index], far, full, columns)
                halves[part, "last", index, unit] = send(far, device(shifted(c, step), core), lines, columns)
                share(far, columns)
    for unit in range(RING):
        for part, (a, b, c, begin, end) in enumerate(PARTS):
            columns = pl.ds(begin, end - begin)
            far = {**shifted(c, 2), a: whole, b: origins(b)[unit]}
            arrived(halves[part, "last", 0, unit], far, low, columns)
            arrived(halves[part, "last", 1, unit], far, high, columns)
            share(far, columns)
    for number, at, columns in sibling_arrivals:
        arrived(number, at, full, columns, 1 - core)
    own_goal.wait()
    for step, copy in enumerate(goal_copies, 1):
        copy.wait_send()
        block = goals_ref.at[(path + paths - step) % paths]
        pltpu.make_async_remote_copy(
            src_ref=block,
            dst_ref=block,
            send_sem=goal_sem.at[step],
            recv_sem=goals_sem.at[step],
            device_id=peers[0],
            device_id_type=pl.DeviceIdType.MESH,
        ).wait_recv()
    for copy in sends:
        copy.wait_send()


COPIES = 156


def gather_tokens(own, goal):
    rows, width = own.shape
    paths, shards = lax.axis_size("path"), lax.axis_size("mp")
    anywhere = pl.BlockSpec(memory_space=pl.ANY)
    out, goals = pl.pallas_call(
        gather_tokens_kernel,
        in_specs=[anywhere, anywhere],
        out_specs=[anywhere, anywhere],
        out_shape=[
            jax.ShapeDtypeStruct((paths // RING, RING, shards // 2, 2, rows, width), own.dtype),
            jax.ShapeDtypeStruct(goal.shape, goal.dtype),
        ],
        scratch_shapes=[
            pltpu.SemaphoreType.DMA,
            pltpu.SemaphoreType.DMA((COPIES,)),
            pltpu.SemaphoreType.DMA((COPIES,)),
            pltpu.SemaphoreType.DMA((paths,)),
            pltpu.SemaphoreType.DMA((paths,)),
        ],
        compiler_params=pltpu.CompilerParams(collective_id=0, has_side_effects=True),
        cost_estimate=pl.CostEstimate(
            flops=0, bytes_accessed=4 * paths * shards * rows * width, transcendentals=0
        ),
        name="gather_tokens",
    )(own, goal)
    return out.reshape(paths * shards * rows, width), goals


def spread_kernel(table_ref, out_ref):
    for g in range(4):
        turned = table_ref[g].T
        out_ref[:, 0, g] = turned.reshape(out_ref.shape[0], out_ref.shape[3], 128)


def spread(table, paths, shards):
    modules, rows, width = table.shape
    groups = modules * rows // 128
    wide = width // shards
    cols = wide // paths
    return pl.pallas_call(
        spread_kernel,
        grid=(shards,),
        in_specs=[pl.BlockSpec((groups, 128, wide), lambda i: (0, 0, i))],
        out_specs=pl.BlockSpec((paths, 1, groups, cols, 128), lambda i: (0, i, 0, 0, 0)),
        out_shape=jax.ShapeDtypeStruct((paths, shards, groups, cols, 128), table.dtype),
        compiler_params=pltpu.CompilerParams(vmem_limit_bytes=VMEM_LIMIT),
        name="spread",
    )(table.reshape(groups, 128, width))


def unspread_kernel(blocks_ref, out_ref):
    for g in range(4):
        out_ref[g] = blocks_ref[:, 0, g].reshape(-1, 128).T


def unspread(blocks, modules, rows):
    paths, shards, groups, cols, _ = blocks.shape
    wide = paths * cols
    out = pl.pallas_call(
        unspread_kernel,
        grid=(shards,),
        in_specs=[pl.BlockSpec((paths, 1, groups, cols, 128), lambda i: (0, i, 0, 0, 0))],
        out_specs=pl.BlockSpec((groups, 128, wide), lambda i: (0, 0, i)),
        out_shape=jax.ShapeDtypeStruct((groups, 128, wide * shards), blocks.dtype),
        compiler_params=pltpu.CompilerParams(vmem_limit_bytes=VMEM_LIMIT),
        name="unspread",
    )(blocks)
    return out.reshape(modules, rows, wide * shards)


def swap_matrix():
    index = jnp.arange(512)
    source, module, row = index // 128, (index // 32) % 4, index % 32
    return (index[:, None] == (module * 128 + source * 32 + row)[None, :]).astype(jnp.bfloat16)


def gather_kernel(blocks_ref, swap_ref, out_ref):
    quads, cols = blocks_ref.shape[0] // 4, blocks_ref.shape[2]
    blocks = blocks_ref[:, 0].reshape(quads, 4, cols, 128)
    line = jnp.concatenate([blocks[:, s].reshape(quads * cols, 128) for s in range(4)], axis=1)
    turned = jnp.dot(line, swap_ref[...], preferred_element_type=jnp.float32).astype(jnp.bfloat16)
    turned = turned.reshape(quads, cols, 512)
    for k in range(quads):
        for q in range(4):
            out_ref[q, :, k * 128 : (k + 1) * 128] = turned[k, :, q * 128 : (q + 1) * 128]


def gather_columns(blocks):
    devices, groups, cols, _ = blocks.shape
    return pl.pallas_call(
        gather_kernel,
        grid=(groups,),
        in_specs=[
            pl.BlockSpec((devices, 1, cols, 128), lambda g: (0, g, 0, 0)),
            pl.BlockSpec((512, 512), lambda g: (0, 0)),
        ],
        out_specs=pl.BlockSpec((4, cols, devices * 32), lambda g: (g, 0, 0)),
        out_shape=jax.ShapeDtypeStruct((groups * 4, cols, devices * 32), blocks.dtype),
        compiler_params=pltpu.CompilerParams(vmem_limit_bytes=VMEM_LIMIT),
        name="gather_columns",
    )(blocks, swap_matrix())


CHUNK = 8


def outer_kernel(counts_ref, sums_ref, table_ref, speed_ref, swap_ref, updated_ref, out_ref):
    group = pl.program_id(0)
    quads, cols = out_ref.shape[0] // 4, out_ref.shape[2]
    counts = [counts_ref[4 * group + q] for q in range(4)]
    for begin in range(0, quads, CHUNK):
        blocks = speed_ref[4 * begin : 4 * (begin + CHUNK), 0].reshape(CHUNK, 4, cols, 128)
        line = jnp.concatenate([blocks[:, s].reshape(CHUNK * cols, 128) for s in range(4)], axis=1)
        speed = jnp.dot(line, swap_ref[...], preferred_element_type=jnp.float32).reshape(CHUNK, cols, 512)
        lines = []
        for k in range(CHUNK):
            pieces_of = []
            for q in range(4):
                columns = slice((begin + k) * 128, (begin + k + 1) * 128)
                average = sums_ref[q, :, columns] / counts[q]
                moment = outer_momentum * speed[k, :, q * 128 : (q + 1) * 128] + average
                begun = table_ref[q, :, columns].astype(jnp.float32)
                updated_ref[q, :, columns] = (
                    begun - outer_rate * (average + outer_momentum * moment)
                ).astype(jnp.bfloat16)
                pieces_of.append(moment.astype(jnp.bfloat16))
            lines.append(jnp.concatenate(pieces_of, axis=1))
        line = jnp.concatenate(lines, axis=0)
        turned = jnp.dot(line, swap_ref[...], preferred_element_type=jnp.float32).astype(jnp.bfloat16)
        turned = turned.reshape(CHUNK, cols, 512)
        for k in range(CHUNK):
            for s in range(4):
                out_ref[4 * (begin + k) + s, 0] = turned[k, :, s * 128 : (s + 1) * 128]


def outer_step(counts, sums, table, speed):
    modules, cols, width = table.shape
    devices, groups = speed.shape[:2]
    rows = pl.BlockSpec((4, cols, width), lambda g: (g, 0, 0))
    blocks = pl.BlockSpec((devices, 1, cols, 128), lambda g: (0, g, 0, 0))
    return pl.pallas_call(
        outer_kernel,
        grid=(groups,),
        in_specs=[
            pl.BlockSpec(memory_space=pltpu.SMEM),
            rows,
            rows,
            blocks,
            pl.BlockSpec((512, 512), lambda g: (0, 0)),
        ],
        out_specs=[rows, blocks],
        out_shape=[
            jax.ShapeDtypeStruct(table.shape, table.dtype),
            jax.ShapeDtypeStruct(speed.shape, speed.dtype),
        ],
        compiler_params=pltpu.CompilerParams(vmem_limit_bytes=VMEM_LIMIT),
        name="outer_step",
    )(counts, sums, table, speed, swap_matrix())


def pieces(value):
    high = value.astype(jnp.bfloat16)
    rest = value - high.astype(jnp.float32)
    middle = rest.astype(jnp.bfloat16)
    low = (rest - middle.astype(jnp.float32)).astype(jnp.bfloat16)
    return jnp.concatenate([high, middle, low], axis=0)


def slopes(weights, normed, goal):
    cols = goal.shape[0]
    both = jnp.dot(weights, normed, preferred_element_type=jnp.float32)
    gate_act, up_act = both[:cols], both[cols:]
    sigma = jax.nn.sigmoid(gate_act)
    swish = gate_act * sigma
    error = (swish * up_act - goal) / TOK_PATH
    d_gate = error * up_act * sigma * (1.0 + gate_act * (1.0 - sigma))
    d_up = error * swish
    return pieces(jnp.concatenate([d_gate, d_up], axis=0))


TILE = 512


def inner_kernel(lists_ref, normed_ref, goal_ref, table_ref, sums_ref, start, current, first_grad, slope, turned):
    path = pl.program_id(0)
    gate, up = lists_ref[2 * path], lists_ref[2 * path + 1]
    cols = goal_ref.shape[1]
    width = normed_ref.shape[1]

    @pl.when(path == 0)
    def _():
        sums_ref[...] = jnp.zeros_like(sums_ref)

    start[:cols] = table_ref[gate]
    start[cols:] = table_ref[up]
    goal = goal_ref[0].astype(jnp.float32)
    for j in range(width // TILE):
        turned[j * TILE : (j + 1) * TILE, :] = normed_ref[:, j * TILE : (j + 1) * TILE].T
    slope[...] = slopes(start[...], turned[...], goal)

    def product(columns):
        parts = jnp.dot(slope[...], normed_ref[:, columns], preferred_element_type=jnp.float32)
        return parts[: 2 * cols] + (parts[2 * cols : 4 * cols] + parts[4 * cols :])

    def after_first(begin, grad):
        return begin - inner_rate * (grad / (jnp.abs(grad) + adam_epsilon) + weight_decay * begin)

    for j in range(width // TILE):
        columns = slice(j * TILE, (j + 1) * TILE)
        grad = product(columns)
        first_grad[:, columns] = grad
        begin = start[:, columns].astype(jnp.float32)
        current[:, columns] = after_first(begin, grad).astype(jnp.bfloat16)

    slope[...] = slopes(current[...], turned[...], goal)
    for j in range(width // TILE):
        columns = slice(j * TILE, (j + 1) * TILE)
        grad = product(columns)
        before = first_grad[:, columns]
        begin = start[:, columns].astype(jnp.float32)
        master = after_first(begin, before)
        first = (beta_first * (1.0 - beta_first) / (1.0 - beta_first**2)) * before + (
            (1.0 - beta_first) / (1.0 - beta_first**2)
        ) * grad
        second = (beta_second * (1.0 - beta_second) / (1.0 - beta_second**2)) * before * before + (
            (1.0 - beta_second) / (1.0 - beta_second**2)
        ) * grad * grad
        master = master - inner_rate * (
            first / (jnp.sqrt(second) + adam_epsilon) + weight_decay * master
        )
        delta = (begin - master).astype(jnp.bfloat16).astype(jnp.float32)
        sums_ref[gate, :, columns] += delta[:cols]
        sums_ref[up, :, columns] += delta[cols:]


def inner_steps(lists, normed, goals, table):
    modules, cols, width = table.shape
    paths = goals.shape[0]
    tokens = normed.shape[0]
    return pl.pallas_call(
        inner_kernel,
        grid_spec=pltpu.PrefetchScalarGridSpec(
            num_scalar_prefetch=1,
            grid=(paths,),
            in_specs=[
                pl.BlockSpec((TOK_PATH, width), lambda p, s: (p, 0)),
                pl.BlockSpec((1, cols, TOK_PATH), lambda p, s: (p, 0, 0)),
                pl.BlockSpec((modules, cols, width), lambda p, s: (0, 0, 0)),
            ],
            out_specs=pl.BlockSpec((modules, cols, width), lambda p, s: (0, 0, 0)),
            scratch_shapes=[
                pltpu.VMEM((2 * cols, width), jnp.bfloat16),
                pltpu.VMEM((2 * cols, width), jnp.bfloat16),
                pltpu.VMEM((2 * cols, width), jnp.float32),
                pltpu.VMEM((6 * cols, TOK_PATH), jnp.bfloat16),
                pltpu.VMEM((width, TOK_PATH), jnp.bfloat16),
            ],
        ),
        out_shape=jax.ShapeDtypeStruct((modules, cols, width), jnp.float32),
        compiler_params=pltpu.CompilerParams(vmem_limit_bytes=VMEM_LIMIT),
        cost_estimate=pl.CostEstimate(
            flops=32 * tokens * width * cols, bytes_accessed=2 * tokens * width, transcendentals=0
        ),
        name="inner_steps",
    )(lists, normed, goals, table)


def evaluate_kernel(lists_ref, normed_ref, table_ref, out_ref, weights, outgoing, arrived, send_sem, recv_sem):
    target = pl.program_id(0)
    path, shard = lax.axis_index("path"), lax.axis_index("mp")
    paths, cols, tokens = arrived.shape

    def remote(block, at, number, other):
        return pltpu.make_async_remote_copy(
            src_ref=outgoing.at[block],
            dst_ref=arrived.at[at],
            send_sem=send_sem.at[block],
            recv_sem=recv_sem.at[number],
            device_id=(other, shard),
            device_id_type=pl.DeviceIdType.MESH,
        )

    @pl.when(target == 0)
    def _():
        barrier = pltpu.get_barrier_semaphore()
        for step in range(1, paths):
            pl.semaphore_signal(
                barrier,
                inc=1,
                device_id=((path + step) % paths, shard),
                device_id_type=pl.DeviceIdType.MESH,
            )
        pl.semaphore_wait(barrier, paths - 1)

    weights[:cols] = table_ref[lists_ref[2 * target]]
    weights[cols:] = table_ref[lists_ref[2 * target + 1]]
    both = lax.dot_general(weights[...], normed_ref[...], NT, preferred_element_type=jnp.float32)
    gate_act = both[:cols]
    result = (gate_act * jax.nn.sigmoid(gate_act) * both[cols:]).astype(jnp.bfloat16)

    @pl.when(target == path)
    def _():
        arrived[path] = result

    @pl.when(target != path)
    def _():
        outgoing[target] = result
        remote(target, path, path, target).start()

    @pl.when(target == paths - 1)
    def _():
        for step in range(1, paths):
            other = (path + step) % paths
            remote(other, other, other, other).wait()
        out_ref[...] = arrived[...].reshape(paths * cols, tokens).T


def evaluate(lists, normed, table):
    modules, cols, width = table.shape
    tokens = normed.shape[0]
    paths = tokens // TOK_PATH
    return pl.pallas_call(
        evaluate_kernel,
        grid=(paths,),
        in_specs=[
            pl.BlockSpec(memory_space=pltpu.SMEM),
            pl.BlockSpec((TOK_PATH, width), lambda p: (p, 0)),
            pl.BlockSpec((modules, cols, width), lambda p: (0, 0, 0)),
        ],
        out_specs=pl.BlockSpec((TOK_PATH, paths * cols), lambda p: (0, 0)),
        scratch_shapes=[
            pltpu.VMEM((2 * cols, width), jnp.bfloat16),
            pltpu.VMEM((paths, cols, TOK_PATH), jnp.bfloat16),
            pltpu.VMEM((paths, cols, TOK_PATH), jnp.bfloat16),
            pltpu.SemaphoreType.DMA((paths,)),
            pltpu.SemaphoreType.DMA((paths,)),
        ],
        out_shape=jax.ShapeDtypeStruct((TOK_PATH, paths * cols), jnp.bfloat16),
        compiler_params=pltpu.CompilerParams(
            vmem_limit_bytes=VMEM_LIMIT, collective_id=1, has_side_effects=True
        ),
        cost_estimate=pl.CostEstimate(
            flops=4 * tokens * width * cols, bytes_accessed=2 * tokens * width, transcendentals=0
        ),
        name="evaluate",
    )(lists, normed, table)


def exchange(blocks, axes):
    return lax.all_to_all(blocks, axes, split_axis=0, concat_axis=0, tiled=True)


def local(features, targets, module_table, momentum, path_lists):
    paths = lax.axis_size("path")
    shards = lax.axis_size("mp")
    modules, rows_own, width = module_table.shape
    cols = width // (paths * shards)
    lists = path_lists.reshape(-1)
    both = ("path", "mp")

    def sent(blocks):
        return exchange(blocks.reshape((paths * shards,) + blocks.shape[-3:]), both)

    own, goal = normalize(features), targets.T.reshape(paths, cols, TOK_PATH)
    speed, module_table, own, goal = lax.optimization_barrier(
        (spread(momentum, paths, shards), spread(module_table, paths, shards), own, goal)
    )
    arrived = sent(module_table)
    normed, goals = gather_tokens(own, goal)
    arrived, normed, speed = lax.optimization_barrier((arrived, normed, speed))
    speed = sent(speed)
    table = gather_columns(arrived)
    select = lists[None, :] == jnp.arange(modules, dtype=jnp.int32)[:, None]
    counts = jnp.sum(select.astype(jnp.float32), axis=1)
    sums = inner_steps(lists, normed, goals, table)
    updated, blocks = lax.optimization_barrier(outer_step(counts, sums, table, speed))
    blocks = sent(blocks)
    evaluated = evaluate(lists, normed, updated)
    momentum_out = unspread(blocks.reshape((paths, shards) + blocks.shape[1:]), modules, rows_own)
    return (momentum_out, evaluated)


def solution(mesh):
    return jax.shard_map(
        local,
        mesh=mesh,
        in_specs=(
            P(("path", "mp"), None),
            P("path", "mp"),
            P(None, ("path", "mp"), None),
            P(None, ("path", "mp"), None),
            P(),
        ),
        out_specs=(P(None, ("path", "mp"), None), P("path", "mp")),
        check_vma=False,
    )
```

```python
import functools

import jax
import jax.numpy as jnp
from jax import lax
from jax.experimental import pallas as pl
from jax.experimental.pallas import tpu as pltpu
from jax.sharding import PartitionSpec as P

TOK_PATH = 512
beta_first = 0.9
beta_second = 0.95
adam_epsilon = 1e-05
inner_rate = 0.004
weight_decay = 0.1
outer_rate = 0.7
outer_momentum = 0.9
VMEM_LIMIT = 56 * 1024 * 1024

NT = (((1,), (1,)), ((), ()))


def normalize(features):
    values = features.astype(jnp.float32)
    factor = lax.rsqrt(jnp.mean(values * values, axis=-1, keepdims=True) + 1e-05)
    return (values * factor).astype(jnp.bfloat16)


RING = 4
PARTS = (("x", "y", "z", 0, 1408), ("y", "z", "x", 1408, 2816), ("z", "x", "y", 2816, 4096))
ARRIVALS = 9


def swap_values():
    source = lax.broadcasted_iota(jnp.int32, (512, 512), 0)
    target = lax.broadcasted_iota(jnp.int32, (512, 512), 1)
    moved = ((source >> 5) & 3) * 128 + (source >> 7) * 32 + (source & 31)
    return (moved == target).astype(jnp.float32).astype(jnp.bfloat16)


def turn_out(rows_ref, blocks_ref, shards, paths):
    groups, cols = blocks_ref.shape[1:3]
    wide = paths * cols

    @pl.loop(0, shards)
    def _(shard):
        columns = pl.ds(pl.multiple_of(shard * wide, wide), wide)
        for g in range(groups):
            turned = rows_ref[g, :, columns].T.reshape(paths, cols, 128)
            for p in range(paths):
                blocks_ref[p * shards + shard, g] = turned[p]


def turn_in(blocks_ref, swap_ref, out_ref):
    devices, groups, cols, _ = blocks_ref.shape
    chunk = 8

    @pl.loop(0, groups)
    def _(g):
        for begin in range(0, devices // 4, chunk):
            blocks = blocks_ref[4 * begin : 4 * (begin + chunk), g].reshape(chunk, 4, cols, 128)
            line = jnp.concatenate([blocks[:, s].reshape(chunk * cols, 128) for s in range(4)], axis=1)
            turned = jnp.dot(line, swap_ref[...], preferred_element_type=jnp.float32)
            turned = turned.astype(jnp.bfloat16).reshape(chunk, cols, 512)
            for k in range(chunk):
                columns = slice((begin + k) * 128, (begin + k + 1) * 128)
                for q in range(4):
                    out_ref[4 * g + q, :, columns] = turned[k, :, q * 128 : (q + 1) * 128]


def gather_tokens_kernel(
    own_ref, goal_ref, rows_ref, speed_ref, out_ref, goals_ref, table_ref, turned_ref,
    rows_in, rows_out, turned, blocks_in, columns_of, swap, local_sem, send_sem, recv_sem, goal_sem, goals_sem, block_sem, blocks_sem, side_sem,
):
    path, shard = lax.axis_index("path"), lax.axis_index("mp")
    me = {"z": path // RING, "y": path % RING, "x": shard // 2}
    core = shard % 2

    def shifted(axis, step):
        return {**me, axis: (me[axis] + (step + RING)) % RING}

    def device(at, which):
        return (at["z"] * RING + at["y"], at["x"] * 2 + which)

    everyone = [device(shifted(axis, step), core) for axis in "xyz" for step in (1, -1)]
    paths, shards = goal_ref.shape[0], out_ref.shape[2] * 2
    peers = [((path + step) % paths, shard) for step in range(1, paths)]
    devices = paths * shards
    mine = path * shards + shard
    load_rows = pltpu.make_async_copy(rows_ref, rows_in, side_sem.at[0])
    load_rows.start()
    barrier = pltpu.get_barrier_semaphore()

    @pl.loop(1, devices)
    def _(step):
        other = (mine + step) % devices
        pl.semaphore_signal(
            barrier, inc=1, device_id=(other // shards, other % shards), device_id_type=pl.DeviceIdType.MESH
        )

    pl.semaphore_wait(barrier, devices - 1)

    whole = pl.ds(0, RING)
    rows = own_ref.shape[0]
    counter = [0]
    sends = []

    def view(at, which, lines, columns):
        return out_ref.at[at["z"], at["y"], at["x"], which, lines, columns]

    def send(at, target, lines, columns, source=None):
        number = counter[0]
        counter[0] += 1
        block = view(at, core, lines, columns)
        copy = pltpu.make_async_remote_copy(
            src_ref=block if source is None else source,
            dst_ref=block,
            send_sem=send_sem.at[number],
            recv_sem=recv_sem.at[number],
            device_id=target,
            device_id_type=pl.DeviceIdType.MESH,
        )
        copy.start()
        sends.append(copy)
        return number

    def arrived(number, at, lines, columns, which=core):
        block = view(at, which, lines, columns)
        pltpu.make_async_remote_copy(
            src_ref=block,
            dst_ref=block,
            send_sem=send_sem.at[number],
            recv_sem=recv_sem.at[number],
            device_id=device(me, 1 - core),
            device_id_type=pl.DeviceIdType.MESH,
        ).wait_recv()

    full, low, high = pl.ds(0, rows), pl.ds(0, rows // 2), pl.ds(rows // 2, rows // 2)
    sibling = device(me, 1 - core)
    sibling_arrivals = []

    def share(at, columns):
        number = send(at, sibling, full, columns)
        sibling_arrivals.append((number, at, columns))

    own_copy = pltpu.make_async_copy(own_ref, view(me, core, full, pl.ds(0, own_ref.shape[1])), local_sem)
    own_copy.start()

    first = {}
    for part, (a, b, c, begin, end) in enumerate(PARTS):
        columns = pl.ds(begin, end - begin)
        source = own_ref.at[:, columns]
        first[part] = [
            send(me, device(shifted(a, step), core), full, columns, source) for step in (1, -1)
        ]
    swap[...] = swap_values()
    load_rows.wait()
    turn_out(rows_in, rows_out, shards, paths)
    own_block = pltpu.make_async_copy(rows_out.at[mine], blocks_in.at[mine], side_sem.at[1])
    own_block.start()

    def exchange_blocks(batch):
        first = batch * BATCH

        @pl.loop(max(first, 1), min(first + BATCH, devices))
        def _(step):
            other = (mine + step) % devices
            pltpu.make_async_remote_copy(
                src_ref=rows_out.at[other],
                dst_ref=blocks_in.at[mine],
                send_sem=block_sem.at[batch],
                recv_sem=blocks_sem.at[batch],
                device_id=(other // shards, other % shards),
                device_id_type=pl.DeviceIdType.MESH,
            ).start()

    def exchanged(batch):
        amount = BATCH - 1 if batch == 0 else BATCH
        return pltpu.make_async_remote_copy(
            src_ref=rows_out.at[pl.ds(0, amount)],
            dst_ref=blocks_in.at[pl.ds(0, amount)],
            send_sem=block_sem.at[batch],
            recv_sem=blocks_sem.at[batch],
            device_id=peers[0],
            device_id_type=pl.DeviceIdType.MESH,
        )

    batches = devices // BATCH

    for batch in range(batches):
        exchange_blocks(batch)
    own_copy.wait()

    own_goal = pltpu.make_async_copy(goal_ref.at[path], goals_ref.at[path], goals_sem.at[0])
    own_goal.start()
    goal_copies = []
    for step, other in enumerate(peers, 1):
        copy = pltpu.make_async_remote_copy(
            src_ref=goal_ref.at[other[0]],
            dst_ref=goals_ref.at[path],
            send_sem=goal_sem.at[step],
            recv_sem=goals_sem.at[step],
            device_id=other,
            device_id_type=pl.DeviceIdType.MESH,
        )
        copy.start()
        goal_copies.append(copy)

    second = {part: [] for part in range(len(PARTS))}

    def send_both(at, axis, columns):
        return [send(at, device(shifted(axis, step), core), full, columns) for step in (1, -1)]

    for part, (a, b, c, begin, end) in enumerate(PARTS):
        second[part].append(send_both(me, b, pl.ds(begin, end - begin)))
    halves = {}
    for index, step in ((0, 1), (1, -1)):
        for part, (a, b, c, begin, end) in enumerate(PARTS):
            columns = pl.ds(begin, end - begin)
            origin = shifted(a, -step)
            arrived(first[part][index], origin, full, columns)
            lines = low if index == 0 else high
            halves[part, index] = send(origin, device(shifted(a, step), core), lines, columns)
            second[part].append(send_both(origin, b, columns))
    for part, (a, b, c, begin, end) in enumerate(PARTS):
        columns = pl.ds(begin, end - begin)
        origin = shifted(a, 2)
        arrived(halves[part, 0], origin, low, columns)
        arrived(halves[part, 1], origin, high, columns)
        second[part].append(send_both(origin, b, columns))

    load_speed = pltpu.make_async_copy(speed_ref, rows_in, side_sem.at[0])
    load_speed.start()

    third = {part: [] for part in range(len(PARTS))}
    for part, (a, b, c, begin, end) in enumerate(PARTS):
        columns = pl.ds(begin, end - begin)
        line = {**me, a: whole}
        third[part].append(send_both(line, c, columns))
        share(line, columns)

    def origins(a):
        return [me[a], (me[a] + 3) % RING, (me[a] + 1) % RING, (me[a] + 2) % RING]

    for index, step in ((0, 1), (1, -1)):
        lines = low if index == 0 else high
        for part, (a, b, c, begin, end) in enumerate(PARTS):
            columns = pl.ds(begin, end - begin)
            far = shifted(b, -step)
            for unit, place in enumerate(origins(a)):
                origin = {**far, a: place}
                arrived(second[part][unit][index], origin, full, columns)
                halves[part, index, unit] = send(origin, device(shifted(b, step), core), lines, columns)
            line = {**far, a: whole}
            third[part].append(send_both(line, c, columns))
            share(line, columns)
    for part, (a, b, c, begin, end) in enumerate(PARTS):
        columns = pl.ds(begin, end - begin)
        far = shifted(b, 2)
        for unit, place in enumerate(origins(a)):
            origin = {**far, a: place}
            arrived(halves[part, 0, unit], origin, low, columns)
            arrived(halves[part, 1, unit], origin, high, columns)
        line = {**far, a: whole}
        third[part].append(send_both(line, c, columns))
        share(line, columns)

    for unit in range(RING):
        if unit == 1:
            load_speed.wait()
            turn_out(rows_in, turned, shards, paths)
            store_speed = pltpu.make_async_copy(turned, turned_ref, side_sem.at[0])
            store_speed.start()
        if unit == 3:
            own_block.wait()
            for batch in range(batches):
                exchanged(batch).wait_recv()
            turn_in(blocks_in, swap, columns_of)
            store_table = pltpu.make_async_copy(columns_of, table_ref, side_sem.at[1])
            store_table.start()
        for index, step in ((0, 1), (1, -1)):
            lines = low if index == 0 else high
            for part, (a, b, c, begin, end) in enumerate(PARTS):
                columns = pl.ds(begin, end - begin)
                far = {**shifted(c, -step), a: whole, b: origins(b)[unit]}
                arrived(third[part][unit][index], far, full, columns)
                halves[part, "last", index, unit] = send(far, device(shifted(c, step), core), lines, columns)
                share(far, columns)
    for unit in range(RING):
        for part, (a, b, c, begin, end) in enumerate(PARTS):
            columns = pl.ds(begin, end - begin)
            far = {**shifted(c, 2), a: whole, b: origins(b)[unit]}
            arrived(halves[part, "last", 0, unit], far, low, columns)
            arrived(halves[part, "last", 1, unit], far, high, columns)
            share(far, columns)
    for number, at, columns in sibling_arrivals:
        arrived(number, at, full, columns, 1 - core)
    for batch in range(batches):
        exchanged(batch).wait_send()
    store_speed.wait()
    store_table.wait()
    own_goal.wait()
    for step, copy in enumerate(goal_copies, 1):
        copy.wait_send()
        block = goals_ref.at[(path + paths - step) % paths]
        pltpu.make_async_remote_copy(
            src_ref=block,
            dst_ref=block,
            send_sem=goal_sem.at[step],
            recv_sem=goals_sem.at[step],
            device_id=peers[0],
            device_id_type=pl.DeviceIdType.MESH,
        ).wait_recv()
    for copy in sends:
        copy.wait_send()


COPIES = 156
BATCH = 16


def gather_tokens(own, goal, table, speed):
    rows, width = own.shape
    modules, rows_own, _ = table.shape
    paths, shards = lax.axis_size("path"), lax.axis_size("mp")
    groups, cols = modules * rows_own // 128, width // (paths * shards)
    anywhere = pl.BlockSpec(memory_space=pl.ANY)
    blocks = (paths * shards, groups, cols, 128)
    out, goals, table, speed = pl.pallas_call(
        gather_tokens_kernel,
        in_specs=[anywhere] * 4,
        out_specs=[anywhere] * 4,
        out_shape=[
            jax.ShapeDtypeStruct((paths // RING, RING, shards // 2, 2, rows, width), own.dtype),
            jax.ShapeDtypeStruct(goal.shape, goal.dtype),
            jax.ShapeDtypeStruct((modules, cols, width), table.dtype),
            jax.ShapeDtypeStruct(blocks, speed.dtype),
        ],
        scratch_shapes=[
            pltpu.VMEM((groups, 128, width), table.dtype),
            pltpu.VMEM(blocks, table.dtype),
            pltpu.VMEM(blocks, table.dtype),
            pltpu.VMEM(blocks, table.dtype),
            pltpu.VMEM((modules, cols, width), table.dtype),
            pltpu.VMEM((512, 512), jnp.bfloat16),
            pltpu.SemaphoreType.DMA,
            pltpu.SemaphoreType.DMA((COPIES,)),
            pltpu.SemaphoreType.DMA((COPIES,)),
            pltpu.SemaphoreType.DMA((paths,)),
            pltpu.SemaphoreType.DMA((paths,)),
            pltpu.SemaphoreType.DMA((paths * shards // BATCH,)),
            pltpu.SemaphoreType.DMA((paths * shards // BATCH,)),
            pltpu.SemaphoreType.DMA((2,)),
        ],
        compiler_params=pltpu.CompilerParams(
            vmem_limit_bytes=VMEM_LIMIT, collective_id=0, has_side_effects=True
        ),
        cost_estimate=pl.CostEstimate(
            flops=0, bytes_accessed=4 * paths * shards * rows * width, transcendentals=0
        ),
        name="gather_tokens",
    )(own, goal, table.reshape(groups, 128, width), speed.reshape(groups, 128, width))
    return out.reshape(paths * shards * rows, width), goals, table, speed


def unspread_kernel(blocks_ref, out_ref):
    for g in range(4):
        out_ref[g] = blocks_ref[:, 0, g].reshape(-1, 128).T


def unspread(blocks, modules, rows):
    paths, shards, groups, cols, _ = blocks.shape
    wide = paths * cols
    out = pl.pallas_call(
        unspread_kernel,
        grid=(shards,),
        in_specs=[pl.BlockSpec((paths, 1, groups, cols, 128), lambda i: (0, i, 0, 0, 0))],
        out_specs=pl.BlockSpec((groups, 128, wide), lambda i: (0, 0, i)),
        out_shape=jax.ShapeDtypeStruct((groups, 128, wide * shards), blocks.dtype),
        compiler_params=pltpu.CompilerParams(vmem_limit_bytes=VMEM_LIMIT),
        name="unspread",
    )(blocks)
    return out.reshape(modules, rows, wide * shards)


def swap_matrix():
    index = jnp.arange(512)
    source, module, row = index // 128, (index // 32) % 4, index % 32
    return (index[:, None] == (module * 128 + source * 32 + row)[None, :]).astype(jnp.bfloat16)


CHUNK = 8


def outer_kernel(counts_ref, sums_ref, table_ref, speed_ref, swap_ref, updated_ref, out_ref):
    group = pl.program_id(0)
    quads, cols = out_ref.shape[0] // 4, out_ref.shape[2]
    counts = [counts_ref[4 * group + q] for q in range(4)]
    for begin in range(0, quads, CHUNK):
        blocks = speed_ref[4 * begin : 4 * (begin + CHUNK), 0].reshape(CHUNK, 4, cols, 128)
        line = jnp.concatenate([blocks[:, s].reshape(CHUNK * cols, 128) for s in range(4)], axis=1)
        speed = jnp.dot(line, swap_ref[...], preferred_element_type=jnp.float32).reshape(CHUNK, cols, 512)
        lines = []
        for k in range(CHUNK):
            pieces_of = []
            for q in range(4):
                columns = slice((begin + k) * 128, (begin + k + 1) * 128)
                average = sums_ref[q, :, columns] / counts[q]
                moment = outer_momentum * speed[k, :, q * 128 : (q + 1) * 128] + average
                begun = table_ref[q, :, columns].astype(jnp.float32)
                updated_ref[q, :, columns] = (
                    begun - outer_rate * (average + outer_momentum * moment)
                ).astype(jnp.bfloat16)
                pieces_of.append(moment.astype(jnp.bfloat16))
            lines.append(jnp.concatenate(pieces_of, axis=1))
        line = jnp.concatenate(lines, axis=0)
        turned = jnp.dot(line, swap_ref[...], preferred_element_type=jnp.float32).astype(jnp.bfloat16)
        turned = turned.reshape(CHUNK, cols, 512)
        for k in range(CHUNK):
            for s in range(4):
                out_ref[4 * (begin + k) + s, 0] = turned[k, :, s * 128 : (s + 1) * 128]


def outer_step(counts, sums, table, speed):
    modules, cols, width = table.shape
    devices, groups = speed.shape[:2]
    rows = pl.BlockSpec((4, cols, width), lambda g: (g, 0, 0))
    blocks = pl.BlockSpec((devices, 1, cols, 128), lambda g: (0, g, 0, 0))
    return pl.pallas_call(
        outer_kernel,
        grid=(groups,),
        in_specs=[
            pl.BlockSpec(memory_space=pltpu.SMEM),
            rows,
            rows,
            blocks,
            pl.BlockSpec((512, 512), lambda g: (0, 0)),
        ],
        out_specs=[rows, blocks],
        out_shape=[
            jax.ShapeDtypeStruct(table.shape, table.dtype),
            jax.ShapeDtypeStruct(speed.shape, speed.dtype),
        ],
        compiler_params=pltpu.CompilerParams(vmem_limit_bytes=VMEM_LIMIT),
        name="outer_step",
    )(counts, sums, table, speed, swap_matrix())


def pieces(value):
    high = value.astype(jnp.bfloat16)
    rest = value - high.astype(jnp.float32)
    middle = rest.astype(jnp.bfloat16)
    low = (rest - middle.astype(jnp.float32)).astype(jnp.bfloat16)
    return jnp.concatenate([high, middle, low], axis=0)


def slopes(weights, normed, goal):
    cols = goal.shape[0]
    both = jnp.dot(weights, normed, preferred_element_type=jnp.float32)
    gate_act, up_act = both[:cols], both[cols:]
    sigma = jax.nn.sigmoid(gate_act)
    swish = gate_act * sigma
    error = (swish * up_act - goal) / TOK_PATH
    d_gate = error * up_act * sigma * (1.0 + gate_act * (1.0 - sigma))
    d_up = error * swish
    return pieces(jnp.concatenate([d_gate, d_up], axis=0))


TILE = 512


def inner_kernel(lists_ref, normed_ref, goal_ref, table_ref, sums_ref, start, current, first_grad, master, slope, turned):
    path = pl.program_id(0)
    gate, up = lists_ref[2 * path], lists_ref[2 * path + 1]
    cols = goal_ref.shape[1]
    width = normed_ref.shape[1]

    @pl.when(path == 0)
    def _():
        sums_ref[...] = jnp.zeros_like(sums_ref)

    start[:cols] = table_ref[gate]
    start[cols:] = table_ref[up]
    goal = goal_ref[0].astype(jnp.float32)
    for j in range(width // 512):
        turned[j * 512 : (j + 1) * 512, :] = normed_ref[:, j * 512 : (j + 1) * 512].T
    slope[...] = slopes(start[...], turned[...], goal)

    def product(columns):
        parts = jnp.dot(slope[...], normed_ref[:, columns], preferred_element_type=jnp.float32)
        return parts[: 2 * cols] + (parts[2 * cols : 4 * cols] + parts[4 * cols :])

    def sweep(update):
        tiles = [slice(j * TILE, (j + 1) * TILE) for j in range(width // TILE)]
        grad = product(tiles[0])
        for this, following in zip(tiles, tiles[1:] + [None]):
            later = product(following) if following is not None else None
            update(this, grad)
            grad = later

    def first_step(columns, grad):
        first_grad[:, columns] = grad
        begin = start[:, columns].astype(jnp.float32)
        after = begin - inner_rate * (grad / (jnp.abs(grad) + adam_epsilon) + weight_decay * begin)
        master[:, columns] = after
        current[:, columns] = after.astype(jnp.bfloat16)

    def second_step(columns, grad):
        before = first_grad[:, columns]
        begin = start[:, columns].astype(jnp.float32)
        after = master[:, columns]
        first = (beta_first * (1.0 - beta_first) / (1.0 - beta_first**2)) * before + (
            (1.0 - beta_first) / (1.0 - beta_first**2)
        ) * grad
        second = (beta_second * (1.0 - beta_second) / (1.0 - beta_second**2)) * before * before + (
            (1.0 - beta_second) / (1.0 - beta_second**2)
        ) * grad * grad
        after = after - inner_rate * (
            first / (jnp.sqrt(second) + adam_epsilon) + weight_decay * after
        )
        delta = (begin - after).astype(jnp.bfloat16).astype(jnp.float32)
        sums_ref[gate, :, columns] += delta[:cols]
        sums_ref[up, :, columns] += delta[cols:]

    sweep(first_step)
    slope[...] = slopes(current[...], turned[...], goal)
    sweep(second_step)


def inner_steps(lists, normed, goals, table):
    modules, cols, width = table.shape
    paths = goals.shape[0]
    tokens = normed.shape[0]
    return pl.pallas_call(
        inner_kernel,
        grid_spec=pltpu.PrefetchScalarGridSpec(
            num_scalar_prefetch=1,
            grid=(paths,),
            in_specs=[
                pl.BlockSpec((TOK_PATH, width), lambda p, s: (p, 0)),
                pl.BlockSpec((1, cols, TOK_PATH), lambda p, s: (p, 0, 0)),
                pl.BlockSpec((modules, cols, width), lambda p, s: (0, 0, 0)),
            ],
            out_specs=pl.BlockSpec((modules, cols, width), lambda p, s: (0, 0, 0)),
            scratch_shapes=[
                pltpu.VMEM((2 * cols, width), jnp.bfloat16),
                pltpu.VMEM((2 * cols, width), jnp.bfloat16),
                pltpu.VMEM((2 * cols, width), jnp.float32),
                pltpu.VMEM((2 * cols, width), jnp.float32),
                pltpu.VMEM((6 * cols, TOK_PATH), jnp.bfloat16),
                pltpu.VMEM((width, TOK_PATH), jnp.bfloat16),
            ],
        ),
        out_shape=jax.ShapeDtypeStruct((modules, cols, width), jnp.float32),
        compiler_params=pltpu.CompilerParams(vmem_limit_bytes=VMEM_LIMIT),
        cost_estimate=pl.CostEstimate(
            flops=32 * tokens * width * cols, bytes_accessed=2 * tokens * width, transcendentals=0
        ),
        name="inner_steps",
    )(lists, normed, goals, table)


def evaluate_kernel(lists_ref, normed_ref, table_ref, out_ref, weights, outgoing, arrived, send_sem, recv_sem):
    target = pl.program_id(0)
    path, shard = lax.axis_index("path"), lax.axis_index("mp")
    paths, cols, tokens = arrived.shape

    def remote(block, at, number, other):
        return pltpu.make_async_remote_copy(
            src_ref=outgoing.at[block],
            dst_ref=arrived.at[at],
            send_sem=send_sem.at[block],
            recv_sem=recv_sem.at[number],
            device_id=(other, shard),
            device_id_type=pl.DeviceIdType.MESH,
        )

    @pl.when(target == 0)
    def _():
        barrier = pltpu.get_barrier_semaphore()
        for step in range(1, paths):
            pl.semaphore_signal(
                barrier,
                inc=1,
                device_id=((path + step) % paths, shard),
                device_id_type=pl.DeviceIdType.MESH,
            )
        pl.semaphore_wait(barrier, paths - 1)

    weights[:cols] = table_ref[lists_ref[2 * target]]
    weights[cols:] = table_ref[lists_ref[2 * target + 1]]
    both = lax.dot_general(weights[...], normed_ref[...], NT, preferred_element_type=jnp.float32)
    gate_act = both[:cols]
    result = (gate_act * jax.nn.sigmoid(gate_act) * both[cols:]).astype(jnp.bfloat16)

    @pl.when(target == path)
    def _():
        arrived[path] = result

    @pl.when(target != path)
    def _():
        outgoing[target] = result
        remote(target, path, path, target).start()

    @pl.when(target == paths - 1)
    def _():
        for step in range(1, paths):
            other = (path + step) % paths
            remote(other, other, other, other).wait()
        out_ref[...] = arrived[...].reshape(paths * cols, tokens).T


def evaluate(lists, normed, table):
    modules, cols, width = table.shape
    tokens = normed.shape[0]
    paths = tokens // TOK_PATH
    return pl.pallas_call(
        evaluate_kernel,
        grid=(paths,),
        in_specs=[
            pl.BlockSpec(memory_space=pltpu.SMEM),
            pl.BlockSpec((TOK_PATH, width), lambda p: (p, 0)),
            pl.BlockSpec((modules, cols, width), lambda p: (0, 0, 0)),
        ],
        out_specs=pl.BlockSpec((TOK_PATH, paths * cols), lambda p: (0, 0)),
        scratch_shapes=[
            pltpu.VMEM((2 * cols, width), jnp.bfloat16),
            pltpu.VMEM((paths, cols, TOK_PATH), jnp.bfloat16),
            pltpu.VMEM((paths, cols, TOK_PATH), jnp.bfloat16),
            pltpu.SemaphoreType.DMA((paths,)),
            pltpu.SemaphoreType.DMA((paths,)),
        ],
        out_shape=jax.ShapeDtypeStruct((TOK_PATH, paths * cols), jnp.bfloat16),
        compiler_params=pltpu.CompilerParams(
            vmem_limit_bytes=VMEM_LIMIT, collective_id=1, has_side_effects=True
        ),
        cost_estimate=pl.CostEstimate(
            flops=4 * tokens * width * cols, bytes_accessed=2 * tokens * width, transcendentals=0
        ),
        name="evaluate",
    )(lists, normed, table)


def exchange(blocks, axes):
    return lax.all_to_all(blocks, axes, split_axis=0, concat_axis=0, tiled=True)


def local(features, targets, module_table, momentum, path_lists):
    paths = lax.axis_size("path")
    shards = lax.axis_size("mp")
    modules, rows_own, width = module_table.shape
    cols = width // (paths * shards)
    lists = path_lists.reshape(-1)
    both = ("path", "mp")

    def sent(blocks):
        return exchange(blocks.reshape((paths * shards,) + blocks.shape[-3:]), both)

    own, goal = normalize(features), targets.T.reshape(paths, cols, TOK_PATH)
    normed, goals, table, speed = gather_tokens(own, goal, module_table, momentum)
    speed = sent(speed)
    select = lists[None, :] == jnp.arange(modules, dtype=jnp.int32)[:, None]
    counts = jnp.sum(select.astype(jnp.float32), axis=1)
    sums = inner_steps(lists, normed, goals, table)
    updated, blocks = lax.optimization_barrier(outer_step(counts, sums, table, speed))
    blocks = sent(blocks)
    evaluated = evaluate(lists, normed, updated)
    momentum_out = unspread(blocks.reshape((paths, shards) + blocks.shape[1:]), modules, rows_own)
    return (momentum_out, evaluated)


def solution(mesh):
    return jax.shard_map(
        local,
        mesh=mesh,
        in_specs=(
            P(("path", "mp"), None),
            P("path", "mp"),
            P(None, ("path", "mp"), None),
            P(None, ("path", "mp"), None),
            P(),
        ),
        out_specs=(P(None, ("path", "mp"), None), P("path", "mp")),
        check_vma=False,
    )
```

```python
import functools

import jax
import jax.numpy as jnp
from jax import lax
from jax.experimental import pallas as pl
from jax.experimental.pallas import tpu as pltpu
from jax.sharding import PartitionSpec as P

TOK_PATH = 512
beta_first = 0.9
beta_second = 0.95
adam_epsilon = 1e-05
inner_rate = 0.004
weight_decay = 0.1
outer_rate = 0.7
outer_momentum = 0.9
VMEM_LIMIT = 56 * 1024 * 1024

NT = (((1,), (1,)), ((), ()))


def normalize(features):
    values = features.astype(jnp.float32)
    factor = lax.rsqrt(jnp.mean(values * values, axis=-1, keepdims=True) + 1e-05)
    return (values * factor).astype(jnp.bfloat16)


RING = 4
PARTS = (("x", "y", "z", 0, 1408), ("y", "z", "x", 1408, 2816), ("z", "x", "y", 2816, 4096))
ARRIVALS = 9


def swap_values():
    source = lax.broadcasted_iota(jnp.int32, (512, 512), 0)
    target = lax.broadcasted_iota(jnp.int32, (512, 512), 1)
    moved = ((source >> 5) & 3) * 128 + (source >> 7) * 32 + (source & 31)
    return (moved == target).astype(jnp.float32).astype(jnp.bfloat16)


def turn_out(rows_ref, blocks_ref, shards, paths):
    groups, cols = blocks_ref.shape[1:3]
    wide = paths * cols

    @pl.loop(0, shards)
    def _(shard):
        columns = pl.ds(pl.multiple_of(shard * wide, wide), wide)
        for g in range(groups):
            turned = rows_ref[g, :, columns].T.reshape(paths, cols, 128)
            for p in range(paths):
                blocks_ref[p * shards + shard, g] = turned[p]


def turn_in(blocks_ref, swap_ref, out_ref):
    devices, groups, cols, _ = blocks_ref.shape
    chunk = 8

    @pl.loop(0, groups)
    def _(g):
        for begin in range(0, devices // 4, chunk):
            blocks = blocks_ref[4 * begin : 4 * (begin + chunk), g].reshape(chunk, 4, cols, 128)
            line = jnp.concatenate([blocks[:, s].reshape(chunk * cols, 128) for s in range(4)], axis=1)
            turned = jnp.dot(line, swap_ref[...], preferred_element_type=jnp.float32)
            turned = turned.astype(jnp.bfloat16).reshape(chunk, cols, 512)
            for k in range(chunk):
                columns = slice((begin + k) * 128, (begin + k + 1) * 128)
                for q in range(4):
                    out_ref[4 * g + q, :, columns] = turned[k, :, q * 128 : (q + 1) * 128]


def gather_tokens_kernel(
    own_ref, goal_ref, rows_ref, speed_ref, out_ref, goals_ref, table_ref, turned_ref,
    rows_in, rows_out, turned, blocks_in, columns_of, swap, local_sem, send_sem, recv_sem, goal_sem, goals_sem, block_sem, blocks_sem, side_sem,
):
    path, shard = lax.axis_index("path"), lax.axis_index("mp")
    me = {"z": path // RING, "y": path % RING, "x": shard // 2}
    core = shard % 2

    def shifted(axis, step):
        return {**me, axis: (me[axis] + (step + RING)) % RING}

    def device(at, which):
        return (at["z"] * RING + at["y"], at["x"] * 2 + which)

    everyone = [device(shifted(axis, step), core) for axis in "xyz" for step in (1, -1)]
    paths, shards = goal_ref.shape[0], out_ref.shape[2] * 2
    peers = [((path + step) % paths, shard) for step in range(1, paths)]
    devices = paths * shards
    mine = path * shards + shard
    load_rows = pltpu.make_async_copy(rows_ref, rows_in, side_sem.at[0])
    load_rows.start()
    barrier = pltpu.get_barrier_semaphore()

    @pl.loop(1, devices)
    def _(step):
        other = (mine + 37 * step) % devices
        pl.semaphore_signal(
            barrier, inc=1, device_id=(other // shards, other % shards), device_id_type=pl.DeviceIdType.MESH
        )

    pl.semaphore_wait(barrier, devices - 1)

    whole = pl.ds(0, RING)
    rows = own_ref.shape[0]
    counter = [0]
    sends = []

    def view(at, which, lines, columns):
        return out_ref.at[at["z"], at["y"], at["x"], which, lines, columns]

    def send(at, target, lines, columns, source=None):
        number = counter[0]
        counter[0] += 1
        block = view(at, core, lines, columns)
        copy = pltpu.make_async_remote_copy(
            src_ref=block if source is None else source,
            dst_ref=block,
            send_sem=send_sem.at[number],
            recv_sem=recv_sem.at[number],
            device_id=target,
            device_id_type=pl.DeviceIdType.MESH,
        )
        copy.start()
        sends.append(copy)
        return number

    def arrived(number, at, lines, columns, which=core):
        block = view(at, which, lines, columns)
        pltpu.make_async_remote_copy(
            src_ref=block,
            dst_ref=block,
            send_sem=send_sem.at[number],
            recv_sem=recv_sem.at[number],
            device_id=device(me, 1 - core),
            device_id_type=pl.DeviceIdType.MESH,
        ).wait_recv()

    full, low, high = pl.ds(0, rows), pl.ds(0, rows // 2), pl.ds(rows // 2, rows // 2)
    sibling = device(me, 1 - core)
    sibling_arrivals = []

    def share(at, columns):
        number = send(at, sibling, full, columns)
        sibling_arrivals.append((number, at, columns))

    own_copy = pltpu.make_async_copy(own_ref, view(me, core, full, pl.ds(0, own_ref.shape[1])), local_sem)
    own_copy.start()

    first = {}
    for part, (a, b, c, begin, end) in enumerate(PARTS):
        columns = pl.ds(begin, end - begin)
        source = own_ref.at[:, columns]
        first[part] = [
            send(me, device(shifted(a, step), core), full, columns, source) for step in (1, -1)
        ]
    swap[...] = swap_values()
    load_rows.wait()
    turn_out(rows_in, rows_out, shards, paths)
    own_block = pltpu.make_async_copy(rows_out.at[mine], blocks_in.at[mine], side_sem.at[1])
    own_block.start()

    def exchange_blocks(batch):
        first = batch * BATCH

        @pl.loop(max(first, 1), min(first + BATCH, devices))
        def _(step):
            other = (mine + 37 * step) % devices
            pltpu.make_async_remote_copy(
                src_ref=rows_out.at[other],
                dst_ref=blocks_in.at[mine],
                send_sem=block_sem.at[batch],
                recv_sem=blocks_sem.at[batch],
                device_id=(other // shards, other % shards),
                device_id_type=pl.DeviceIdType.MESH,
            ).start()

    def exchanged(batch):
        amount = BATCH - 1 if batch == 0 else BATCH
        return pltpu.make_async_remote_copy(
            src_ref=rows_out.at[pl.ds(0, amount)],
            dst_ref=blocks_in.at[pl.ds(0, amount)],
            send_sem=block_sem.at[batch],
            recv_sem=blocks_sem.at[batch],
            device_id=peers[0],
            device_id_type=pl.DeviceIdType.MESH,
        )

    batches = devices // BATCH

    for batch in range(batches):
        exchange_blocks(batch)
    own_copy.wait()

    own_goal = pltpu.make_async_copy(goal_ref.at[path], goals_ref.at[path], goals_sem.at[0])
    own_goal.start()
    goal_copies = []
    for step, other in enumerate(peers, 1):
        copy = pltpu.make_async_remote_copy(
            src_ref=goal_ref.at[other[0]],
            dst_ref=goals_ref.at[path],
            send_sem=goal_sem.at[step],
            recv_sem=goals_sem.at[step],
            device_id=other,
            device_id_type=pl.DeviceIdType.MESH,
        )
        copy.start()
        goal_copies.append(copy)

    second = {part: [] for part in range(len(PARTS))}

    def send_both(at, axis, columns):
        return [send(at, device(shifted(axis, step), core), full, columns) for step in (1, -1)]

    for part, (a, b, c, begin, end) in enumerate(PARTS):
        second[part].append(send_both(me, b, pl.ds(begin, end - begin)))
    halves = {}
    for index, step in ((0, 1), (1, -1)):
        for part, (a, b, c, begin, end) in enumerate(PARTS):
            columns = pl.ds(begin, end - begin)
            origin = shifted(a, -step)
            arrived(first[part][index], origin, full, columns)
            lines = low if index == 0 else high
            halves[part, index] = send(origin, device(shifted(a, step), core), lines, columns)
            second[part].append(send_both(origin, b, columns))
    for part, (a, b, c, begin, end) in enumerate(PARTS):
        columns = pl.ds(begin, end - begin)
        origin = shifted(a, 2)
        arrived(halves[part, 0], origin, low, columns)
        arrived(halves[part, 1], origin, high, columns)
        second[part].append(send_both(origin, b, columns))

    load_speed = pltpu.make_async_copy(speed_ref, rows_in, side_sem.at[0])
    load_speed.start()

    third = {part: [] for part in range(len(PARTS))}
    for part, (a, b, c, begin, end) in enumerate(PARTS):
        columns = pl.ds(begin, end - begin)
        line = {**me, a: whole}
        third[part].append(send_both(line, c, columns))
        share(line, columns)

    def origins(a):
        return [me[a], (me[a] + 3) % RING, (me[a] + 1) % RING, (me[a] + 2) % RING]

    for index, step in ((0, 1), (1, -1)):
        lines = low if index == 0 else high
        for part, (a, b, c, begin, end) in enumerate(PARTS):
            columns = pl.ds(begin, end - begin)
            far = shifted(b, -step)
            for unit, place in enumerate(origins(a)):
                origin = {**far, a: place}
                arrived(second[part][unit][index], origin, full, columns)
                halves[part, index, unit] = send(origin, device(shifted(b, step), core), lines, columns)
            line = {**far, a: whole}
            third[part].append(send_both(line, c, columns))
            share(line, columns)
    for part, (a, b, c, begin, end) in enumerate(PARTS):
        columns = pl.ds(begin, end - begin)
        far = shifted(b, 2)
        for unit, place in enumerate(origins(a)):
            origin = {**far, a: place}
            arrived(halves[part, 0, unit], origin, low, columns)
            arrived(halves[part, 1, unit], origin, high, columns)
        line = {**far, a: whole}
        third[part].append(send_both(line, c, columns))
        share(line, columns)

    for unit in range(RING):
        if unit == 1:
            load_speed.wait()
            turn_out(rows_in, turned, shards, paths)
            store_speed = pltpu.make_async_copy(turned, turned_ref, side_sem.at[0])
            store_speed.start()
        if unit == 3:
            own_block.wait()
            for batch in range(batches):
                exchanged(batch).wait_recv()
            turn_in(blocks_in, swap, columns_of)
            store_table = pltpu.make_async_copy(columns_of, table_ref, side_sem.at[1])
            store_table.start()
        for index, step in ((0, 1), (1, -1)):
            lines = low if index == 0 else high
            for part, (a, b, c, begin, end) in enumerate(PARTS):
                columns = pl.ds(begin, end - begin)
                far = {**shifted(c, -step), a: whole, b: origins(b)[unit]}
                arrived(third[part][unit][index], far, full, columns)
                halves[part, "last", index, unit] = send(far, device(shifted(c, step), core), lines, columns)
                share(far, columns)
    for unit in range(RING):
        for part, (a, b, c, begin, end) in enumerate(PARTS):
            columns = pl.ds(begin, end - begin)
            far = {**shifted(c, 2), a: whole, b: origins(b)[unit]}
            arrived(halves[part, "last", 0, unit], far, low, columns)
            arrived(halves[part, "last", 1, unit], far, high, columns)
            share(far, columns)
    for number, at, columns in sibling_arrivals:
        arrived(number, at, full, columns, 1 - core)
    for batch in range(batches):
        exchanged(batch).wait_send()
    store_speed.wait()
    store_table.wait()
    own_goal.wait()
    for step, copy in enumerate(goal_copies, 1):
        copy.wait_send()
        block = goals_ref.at[(path + paths - step) % paths]
        pltpu.make_async_remote_copy(
            src_ref=block,
            dst_ref=block,
            send_sem=goal_sem.at[step],
            recv_sem=goals_sem.at[step],
            device_id=peers[0],
            device_id_type=pl.DeviceIdType.MESH,
        ).wait_recv()
    for copy in sends:
        copy.wait_send()


COPIES = 156
BATCH = 16


def gather_tokens(own, goal, table, speed):
    rows, width = own.shape
    modules, rows_own, _ = table.shape
    paths, shards = lax.axis_size("path"), lax.axis_size("mp")
    groups, cols = modules * rows_own // 128, width // (paths * shards)
    anywhere = pl.BlockSpec(memory_space=pl.ANY)
    blocks = (paths * shards, groups, cols, 128)
    out, goals, table, speed = pl.pallas_call(
        gather_tokens_kernel,
        in_specs=[anywhere] * 4,
        out_specs=[anywhere] * 4,
        out_shape=[
            jax.ShapeDtypeStruct((paths // RING, RING, shards // 2, 2, rows, width), own.dtype),
            jax.ShapeDtypeStruct(goal.shape, goal.dtype),
            jax.ShapeDtypeStruct((modules, cols, width), table.dtype),
            jax.ShapeDtypeStruct(blocks, speed.dtype),
        ],
        scratch_shapes=[
            pltpu.VMEM((groups, 128, width), table.dtype),
            pltpu.VMEM(blocks, table.dtype),
            pltpu.VMEM(blocks, table.dtype),
            pltpu.VMEM(blocks, table.dtype),
            pltpu.VMEM((modules, cols, width), table.dtype),
            pltpu.VMEM((512, 512), jnp.bfloat16),
            pltpu.SemaphoreType.DMA,
            pltpu.SemaphoreType.DMA((COPIES,)),
            pltpu.SemaphoreType.DMA((COPIES,)),
            pltpu.SemaphoreType.DMA((paths,)),
            pltpu.SemaphoreType.DMA((paths,)),
            pltpu.SemaphoreType.DMA((paths * shards // BATCH,)),
            pltpu.SemaphoreType.DMA((paths * shards // BATCH,)),
            pltpu.SemaphoreType.DMA((2,)),
        ],
        compiler_params=pltpu.CompilerParams(
            vmem_limit_bytes=VMEM_LIMIT, collective_id=0, has_side_effects=True
        ),
        cost_estimate=pl.CostEstimate(
            flops=0, bytes_accessed=4 * paths * shards * rows * width, transcendentals=0
        ),
        name="gather_tokens",
    )(own, goal, table.reshape(groups, 128, width), speed.reshape(groups, 128, width))
    return out.reshape(paths * shards * rows, width), goals, table, speed


def unspread_kernel(blocks_ref, out_ref):
    for g in range(4):
        out_ref[g] = blocks_ref[:, 0, g].reshape(-1, 128).T


def unspread(blocks, modules, rows):
    paths, shards, groups, cols, _ = blocks.shape
    wide = paths * cols
    out = pl.pallas_call(
        unspread_kernel,
        grid=(shards,),
        in_specs=[pl.BlockSpec((paths, 1, groups, cols, 128), lambda i: (0, i, 0, 0, 0))],
        out_specs=pl.BlockSpec((groups, 128, wide), lambda i: (0, 0, i)),
        out_shape=jax.ShapeDtypeStruct((groups, 128, wide * shards), blocks.dtype),
        compiler_params=pltpu.CompilerParams(vmem_limit_bytes=VMEM_LIMIT),
        name="unspread",
    )(blocks)
    return out.reshape(modules, rows, wide * shards)


def swap_matrix():
    index = jnp.arange(512)
    source, module, row = index // 128, (index // 32) % 4, index % 32
    return (index[:, None] == (module * 128 + source * 32 + row)[None, :]).astype(jnp.bfloat16)


CHUNK = 8


def outer_step(counts_ref, sums_ref, table_ref, speed_ref, swap_ref, updated_ref, out_ref, group):
    quads, cols = out_ref.shape[0] // 4, out_ref.shape[2]
    counts = [counts_ref[4 * group + q] for q in range(4)]
    for begin in range(0, quads, CHUNK):
        blocks = speed_ref[4 * begin : 4 * (begin + CHUNK), group].reshape(CHUNK, 4, cols, 128)
        line = jnp.concatenate([blocks[:, s].reshape(CHUNK * cols, 128) for s in range(4)], axis=1)
        speed = jnp.dot(line, swap_ref[...], preferred_element_type=jnp.float32).reshape(CHUNK, cols, 512)
        lines = []
        for k in range(CHUNK):
            moments = []
            for q in range(4):
                columns = slice((begin + k) * 128, (begin + k + 1) * 128)
                average = sums_ref[4 * group + q, :, columns] / counts[q]
                moment = outer_momentum * speed[k, :, q * 128 : (q + 1) * 128] + average
                begun = table_ref[4 * group + q, :, columns].astype(jnp.float32)
                updated_ref[4 * group + q, :, columns] = (
                    begun - outer_rate * (average + outer_momentum * moment)
                ).astype(jnp.bfloat16)
                moments.append(moment.astype(jnp.bfloat16))
            lines.append(jnp.concatenate(moments, axis=1))
        line = jnp.concatenate(lines, axis=0)
        turned = jnp.dot(line, swap_ref[...], preferred_element_type=jnp.float32).astype(jnp.bfloat16)
        turned = turned.reshape(CHUNK, cols, 512)
        for k in range(CHUNK):
            for s in range(4):
                out_ref[4 * (begin + k) + s, group] = turned[k, :, s * 128 : (s + 1) * 128]


def pieces(value):
    high = value.astype(jnp.bfloat16)
    rest = value - high.astype(jnp.float32)
    middle = rest.astype(jnp.bfloat16)
    low = (rest - middle.astype(jnp.float32)).astype(jnp.bfloat16)
    return jnp.concatenate([high, middle, low], axis=0)


def slopes(weights, normed, goal):
    cols = goal.shape[0]
    both = jnp.dot(weights, normed, preferred_element_type=jnp.float32)
    gate_act, up_act = both[:cols], both[cols:]
    sigma = jax.nn.sigmoid(gate_act)
    swish = gate_act * sigma
    error = (swish * up_act - goal) / TOK_PATH
    d_gate = error * up_act * sigma * (1.0 + gate_act * (1.0 - sigma))
    d_up = error * swish
    return pieces(jnp.concatenate([d_gate, d_up], axis=0))


TILE = 512


def inner_kernel(lists_ref, normed_ref, goal_ref, table_ref, sums_ref, start, current, first_grad, master, slope, turned):
    path = pl.program_id(0)
    gate, up = lists_ref[2 * path], lists_ref[2 * path + 1]
    cols = goal_ref.shape[1]
    width = normed_ref.shape[1]

    @pl.when(path == 0)
    def _():
        sums_ref[...] = jnp.zeros_like(sums_ref)

    start[:cols] = table_ref[gate]
    start[cols:] = table_ref[up]
    goal = goal_ref[0].astype(jnp.float32)
    for j in range(width // 512):
        turned[j * 512 : (j + 1) * 512, :] = normed_ref[:, j * 512 : (j + 1) * 512].T
    slope[...] = slopes(start[...], turned[...], goal)

    def product(columns):
        parts = jnp.dot(slope[...], normed_ref[:, columns], preferred_element_type=jnp.float32)
        return parts[: 2 * cols] + (parts[2 * cols : 4 * cols] + parts[4 * cols :])

    def sweep(update):
        tiles = [slice(j * TILE, (j + 1) * TILE) for j in range(width // TILE)]
        grad = product(tiles[0])
        for this, following in zip(tiles, tiles[1:] + [None]):
            later = product(following) if following is not None else None
            update(this, grad)
            grad = later

    def first_step(columns, grad):
        first_grad[:, columns] = grad
        begin = start[:, columns].astype(jnp.float32)
        after = begin - inner_rate * (grad / (jnp.abs(grad) + adam_epsilon) + weight_decay * begin)
        master[:, columns] = after
        current[:, columns] = after.astype(jnp.bfloat16)

    def second_step(columns, grad):
        before = first_grad[:, columns]
        begin = start[:, columns].astype(jnp.float32)
        after = master[:, columns]
        first = (beta_first * (1.0 - beta_first) / (1.0 - beta_first**2)) * before + (
            (1.0 - beta_first) / (1.0 - beta_first**2)
        ) * grad
        second = (beta_second * (1.0 - beta_second) / (1.0 - beta_second**2)) * before * before + (
            (1.0 - beta_second) / (1.0 - beta_second**2)
        ) * grad * grad
        after = after - inner_rate * (
            first / (jnp.sqrt(second) + adam_epsilon) + weight_decay * after
        )
        delta = (begin - after).astype(jnp.bfloat16).astype(jnp.float32)
        sums_ref[gate, :, columns] += delta[:cols]
        sums_ref[up, :, columns] += delta[cols:]

    sweep(first_step)
    slope[...] = slopes(current[...], turned[...], goal)
    sweep(second_step)


def inner_steps(lists, normed, goals, table):
    modules, cols, width = table.shape
    paths = goals.shape[0]
    tokens = normed.shape[0]
    return pl.pallas_call(
        inner_kernel,
        grid_spec=pltpu.PrefetchScalarGridSpec(
            num_scalar_prefetch=1,
            grid=(paths,),
            in_specs=[
                pl.BlockSpec((TOK_PATH, width), lambda p, s: (p, 0)),
                pl.BlockSpec((1, cols, TOK_PATH), lambda p, s: (p, 0, 0)),
                pl.BlockSpec((modules, cols, width), lambda p, s: (0, 0, 0)),
            ],
            out_specs=pl.BlockSpec((modules, cols, width), lambda p, s: (0, 0, 0)),
            scratch_shapes=[
                pltpu.VMEM((2 * cols, width), jnp.bfloat16),
                pltpu.VMEM((2 * cols, width), jnp.bfloat16),
                pltpu.VMEM((2 * cols, width), jnp.float32),
                pltpu.VMEM((2 * cols, width), jnp.float32),
                pltpu.VMEM((6 * cols, TOK_PATH), jnp.bfloat16),
                pltpu.VMEM((width, TOK_PATH), jnp.bfloat16),
            ],
        ),
        out_shape=jax.ShapeDtypeStruct((modules, cols, width), jnp.float32),
        compiler_params=pltpu.CompilerParams(vmem_limit_bytes=VMEM_LIMIT),
        cost_estimate=pl.CostEstimate(
            flops=32 * tokens * width * cols, bytes_accessed=2 * tokens * width, transcendentals=0
        ),
        name="inner_steps",
    )(lists, normed, goals, table)


def finish_kernel(
    lists_ref, counts_ref, normed_ref, sums_ref, table_ref, speed_ref, moments_ref, out_ref,
    sums, begun, speed, updated, blocks_out, blocks_in, swap, weights, outgoing, arrived,
    send_sem, recv_sem, block_sem, blocks_sem, sums_sem, side_sem,
):
    target = pl.program_id(0)
    path, shard = lax.axis_index("path"), lax.axis_index("mp")
    paths, cols, tokens = arrived.shape

    def remote(block, at, number, other):
        return pltpu.make_async_remote_copy(
            src_ref=outgoing.at[block],
            dst_ref=arrived.at[at],
            send_sem=send_sem.at[block],
            recv_sem=recv_sem.at[number],
            device_id=(other, shard),
            device_id_type=pl.DeviceIdType.MESH,
        )

    devices, groups = blocks_out.shape[:2]
    shards = devices // paths
    mine = path * shards + shard
    batches = devices // BATCH

    def exchanged(batch):
        amount = BATCH - 1 if batch == 0 else BATCH
        return pltpu.make_async_remote_copy(
            src_ref=blocks_out.at[pl.ds(0, amount)],
            dst_ref=blocks_in.at[pl.ds(0, amount)],
            send_sem=block_sem.at[batch],
            recv_sem=blocks_sem.at[batch],
            device_id=((path + 1) % paths, shard),
            device_id_type=pl.DeviceIdType.MESH,
        )

    def own_block():
        return pltpu.make_async_copy(blocks_out.at[mine], blocks_in.at[mine], side_sem.at[0])

    @pl.when(target == 0)
    def _():
        load_table = pltpu.make_async_copy(table_ref, begun, side_sem.at[0])
        load_speed = pltpu.make_async_copy(speed_ref, speed, side_sem.at[1])
        load_speed.start()
        load_table.start()
        loads = []
        for g in range(groups):
            part = pl.ds(4 * g, 4)
            loads.append(pltpu.make_async_copy(sums_ref.at[part], sums.at[part], sums_sem.at[g]))
            loads[-1].start()
        barrier = pltpu.get_barrier_semaphore()

        @pl.loop(1, devices)
        def _(step):
            other = (mine + 37 * step) % devices
            pl.semaphore_signal(
                barrier, inc=1, device_id=(other // shards, other % shards), device_id_type=pl.DeviceIdType.MESH
            )

        swap[...] = swap_values()
        load_speed.wait()
        load_table.wait()
        for load in loads:
            load.wait()

        @pl.loop(0, groups)
        def _(group):
            outer_step(counts_ref, sums, begun, speed, swap, updated, blocks_out, group)

        own_block().start()
        pl.semaphore_wait(barrier, devices - 1)
        for batch in range(batches):

            @pl.loop(max(batch * BATCH, 1), (batch + 1) * BATCH)
            def _(step):
                other = (mine + 37 * step) % devices
                pltpu.make_async_remote_copy(
                    src_ref=blocks_out.at[other],
                    dst_ref=blocks_in.at[mine],
                    send_sem=block_sem.at[batch],
                    recv_sem=blocks_sem.at[batch],
                    device_id=(other // shards, other % shards),
                    device_id_type=pl.DeviceIdType.MESH,
                ).start()

    weights[:cols] = updated[lists_ref[2 * target]]
    weights[cols:] = updated[lists_ref[2 * target + 1]]
    both = lax.dot_general(weights[...], normed_ref[...], NT, preferred_element_type=jnp.float32)
    gate_act = both[:cols]
    result = (gate_act * jax.nn.sigmoid(gate_act) * both[cols:]).astype(jnp.bfloat16)

    @pl.when(target == path)
    def _():
        arrived[path] = result

    @pl.when(target != path)
    def _():
        outgoing[target] = result
        remote(target, path, path, target).start()

    @pl.when(target == paths - 1)
    def _():
        for step in range(1, paths):
            other = (path + step) % paths
            remote(other, other, other, other).wait()
        out_ref[...] = arrived[...].reshape(paths * cols, tokens).T
        own_block().wait()
        for batch in range(batches):
            exchanged(batch).wait()
        store = pltpu.make_async_copy(blocks_in, moments_ref, side_sem.at[0])
        store.start()
        store.wait()


def finish(lists, counts, normed, sums, table, speed):
    modules, cols, width = table.shape
    tokens = normed.shape[0]
    paths = tokens // TOK_PATH
    scalars, anywhere = pl.BlockSpec(memory_space=pltpu.SMEM), pl.BlockSpec(memory_space=pl.ANY)
    return pl.pallas_call(
        finish_kernel,
        grid=(paths,),
        in_specs=[
            scalars,
            scalars,
            pl.BlockSpec((TOK_PATH, width), lambda p: (p, 0)),
            anywhere,
            anywhere,
            anywhere,
        ],
        out_specs=[anywhere, pl.BlockSpec((TOK_PATH, paths * cols), lambda p: (0, 0))],
        scratch_shapes=[
            pltpu.VMEM(sums.shape, sums.dtype),
            pltpu.VMEM(table.shape, table.dtype),
            pltpu.VMEM(speed.shape, speed.dtype),
            pltpu.VMEM(table.shape, table.dtype),
            pltpu.VMEM(speed.shape, speed.dtype),
            pltpu.VMEM(speed.shape, speed.dtype),
            pltpu.VMEM((512, 512), jnp.bfloat16),
            pltpu.VMEM((2 * cols, width), jnp.bfloat16),
            pltpu.VMEM((paths, cols, TOK_PATH), jnp.bfloat16),
            pltpu.VMEM((paths, cols, TOK_PATH), jnp.bfloat16),
            pltpu.SemaphoreType.DMA((paths,)),
            pltpu.SemaphoreType.DMA((paths,)),
            pltpu.SemaphoreType.DMA((speed.shape[0] // BATCH,)),
            pltpu.SemaphoreType.DMA((speed.shape[0] // BATCH,)),
            pltpu.SemaphoreType.DMA((speed.shape[1],)),
            pltpu.SemaphoreType.DMA((2,)),
        ],
        out_shape=[
            jax.ShapeDtypeStruct(speed.shape, speed.dtype),
            jax.ShapeDtypeStruct((TOK_PATH, paths * cols), jnp.bfloat16),
        ],
        compiler_params=pltpu.CompilerParams(
            vmem_limit_bytes=VMEM_LIMIT, collective_id=1, has_side_effects=True
        ),
        cost_estimate=pl.CostEstimate(
            flops=4 * tokens * width * cols, bytes_accessed=2 * tokens * width, transcendentals=0
        ),
        name="finish",
    )(lists, counts, normed, sums, table, speed)


def exchange(blocks, axes):
    return lax.all_to_all(blocks, axes, split_axis=0, concat_axis=0, tiled=True)


def local(features, targets, module_table, momentum, path_lists):
    paths = lax.axis_size("path")
    shards = lax.axis_size("mp")
    modules, rows_own, width = module_table.shape
    cols = width // (paths * shards)
    lists = path_lists.reshape(-1)
    both = ("path", "mp")

    def sent(blocks):
        return exchange(blocks.reshape((paths * shards,) + blocks.shape[-3:]), both)

    own, goal = normalize(features), targets.T.reshape(paths, cols, TOK_PATH)
    normed, goals, table, speed = gather_tokens(own, goal, module_table, momentum)
    speed = sent(speed)
    select = lists[None, :] == jnp.arange(modules, dtype=jnp.int32)[:, None]
    counts = jnp.sum(select.astype(jnp.float32), axis=1)
    sums = inner_steps(lists, normed, goals, table)
    blocks, evaluated = finish(lists, counts, normed, sums, table, speed)
    momentum_out = unspread(blocks.reshape((paths, shards) + blocks.shape[1:]), modules, rows_own)
    return (momentum_out, evaluated)


def solution(mesh):
    return jax.shard_map(
        local,
        mesh=mesh,
        in_specs=(
            P(("path", "mp"), None),
            P("path", "mp"),
            P(None, ("path", "mp"), None),
            P(None, ("path", "mp"), None),
            P(),
        ),
        out_specs=(P(None, ("path", "mp"), None), P("path", "mp")),
        check_vma=False,
    )
```

```python
import functools

import jax
import jax.numpy as jnp
from jax import lax
from jax.experimental import pallas as pl
from jax.experimental.pallas import tpu as pltpu
from jax.sharding import PartitionSpec as P

TOK_PATH = 512
beta_first = 0.9
beta_second = 0.95
adam_epsilon = 1e-05
inner_rate = 0.004
weight_decay = 0.1
outer_rate = 0.7
outer_momentum = 0.9
VMEM_LIMIT = 56 * 1024 * 1024

NT = (((1,), (1,)), ((), ()))


def normalize(features):
    values = features.astype(jnp.float32)
    factor = lax.rsqrt(jnp.mean(values * values, axis=-1, keepdims=True) + 1e-05)
    return (values * factor).astype(jnp.bfloat16)


RING = 4
PARTS = (("x", "y", "z", 0, 1408), ("y", "z", "x", 1408, 2816), ("z", "x", "y", 2816, 4096))
ARRIVALS = 9


def swap_values():
    source = lax.broadcasted_iota(jnp.int32, (512, 512), 0)
    target = lax.broadcasted_iota(jnp.int32, (512, 512), 1)
    moved = ((source >> 5) & 3) * 128 + (source >> 7) * 32 + (source & 31)
    return (moved == target).astype(jnp.float32).astype(jnp.bfloat16)


def turn_out(rows_ref, blocks_ref, shards, paths):
    groups, cols = blocks_ref.shape[1:3]
    wide = paths * cols

    @pl.loop(0, shards)
    def _(shard):
        columns = pl.ds(pl.multiple_of(shard * wide, wide), wide)
        for g in range(groups):
            turned = rows_ref[g, :, columns].T.reshape(paths, cols, 128)
            for p in range(paths):
                blocks_ref[p * shards + shard, g] = turned[p]


def turn_in(blocks_ref, swap_ref, out_ref):
    devices, groups, cols, _ = blocks_ref.shape
    chunk = 8

    @pl.loop(0, groups)
    def _(g):
        for begin in range(0, devices // 4, chunk):
            blocks = blocks_ref[4 * begin : 4 * (begin + chunk), g].reshape(chunk, 4, cols, 128)
            line = jnp.concatenate([blocks[:, s].reshape(chunk * cols, 128) for s in range(4)], axis=1)
            turned = jnp.dot(line, swap_ref[...], preferred_element_type=jnp.float32)
            turned = turned.astype(jnp.bfloat16).reshape(chunk, cols, 512)
            for k in range(chunk):
                columns = slice((begin + k) * 128, (begin + k + 1) * 128)
                for q in range(4):
                    out_ref[4 * g + q, :, columns] = turned[k, :, q * 128 : (q + 1) * 128]


def gather_tokens_kernel(
    own_ref, goal_ref, rows_ref, speed_ref, out_ref, goals_ref, table_ref, turned_ref,
    rows_in, rows_out, turned, blocks_in, columns_of, swap, local_sem, send_sem, recv_sem, goal_sem, goals_sem, block_sem, blocks_sem, side_sem,
):
    path, shard = lax.axis_index("path"), lax.axis_index("mp")
    me = {"z": path // RING, "y": path % RING, "x": shard // 2}
    core = shard % 2

    def shifted(axis, step):
        return {**me, axis: (me[axis] + (step + RING)) % RING}

    def device(at, which):
        return (at["z"] * RING + at["y"], at["x"] * 2 + which)

    everyone = [device(shifted(axis, step), core) for axis in "xyz" for step in (1, -1)]
    paths, shards = goal_ref.shape[0], out_ref.shape[2] * 2
    peers = [((path + step) % paths, shard) for step in range(1, paths)]
    devices = paths * shards
    mine = path * shards + shard
    load_rows = pltpu.make_async_copy(rows_ref, rows_in, side_sem.at[0])
    load_rows.start()
    barrier = pltpu.get_barrier_semaphore()

    @pl.loop(1, devices)
    def _(step):
        other = (mine + 45 * step) % devices
        pl.semaphore_signal(
            barrier, inc=1, device_id=(other // shards, other % shards), device_id_type=pl.DeviceIdType.MESH
        )

    pl.semaphore_wait(barrier, devices - 1)

    whole = pl.ds(0, RING)
    rows = own_ref.shape[0]
    counter = [0]
    sends = []

    def view(at, which, lines, columns):
        return out_ref.at[at["z"], at["y"], at["x"], which, lines, columns]

    def send(at, target, lines, columns, source=None):
        number = counter[0]
        counter[0] += 1
        block = view(at, core, lines, columns)
        copy = pltpu.make_async_remote_copy(
            src_ref=block if source is None else source,
            dst_ref=block,
            send_sem=send_sem.at[number],
            recv_sem=recv_sem.at[number],
            device_id=target,
            device_id_type=pl.DeviceIdType.MESH,
        )
        copy.start()
        sends.append(copy)
        return number

    def arrived(number, at, lines, columns, which=core):
        block = view(at, which, lines, columns)
        pltpu.make_async_remote_copy(
            src_ref=block,
            dst_ref=block,
            send_sem=send_sem.at[number],
            recv_sem=recv_sem.at[number],
            device_id=device(me, 1 - core),
            device_id_type=pl.DeviceIdType.MESH,
        ).wait_recv()

    full, low, high = pl.ds(0, rows), pl.ds(0, rows // 2), pl.ds(rows // 2, rows // 2)
    sibling = device(me, 1 - core)
    sibling_arrivals = []

    def share(at, columns):
        number = send(at, sibling, full, columns)
        sibling_arrivals.append((number, at, columns))

    own_copy = pltpu.make_async_copy(own_ref, view(me, core, full, pl.ds(0, own_ref.shape[1])), local_sem)
    own_copy.start()

    first = {}
    for part, (a, b, c, begin, end) in enumerate(PARTS):
        columns = pl.ds(begin, end - begin)
        source = own_ref.at[:, columns]
        first[part] = [
            send(me, device(shifted(a, step), core), full, columns, source) for step in (1, -1)
        ]
    swap[...] = swap_values()
    load_rows.wait()
    turn_out(rows_in, rows_out, shards, paths)
    own_block = pltpu.make_async_copy(rows_out.at[mine], blocks_in.at[mine], side_sem.at[1])
    own_block.start()

    def exchange_blocks(batch):
        first = batch * BATCH

        @pl.loop(max(first, 1), min(first + BATCH, devices))
        def _(step):
            other = (mine + 45 * step) % devices
            pltpu.make_async_remote_copy(
                src_ref=rows_out.at[other],
                dst_ref=blocks_in.at[mine],
                send_sem=block_sem.at[batch],
                recv_sem=blocks_sem.at[batch],
                device_id=(other // shards, other % shards),
                device_id_type=pl.DeviceIdType.MESH,
            ).start()

    def exchanged(batch):
        amount = BATCH - 1 if batch == 0 else BATCH
        return pltpu.make_async_remote_copy(
            src_ref=rows_out.at[pl.ds(0, amount)],
            dst_ref=blocks_in.at[pl.ds(0, amount)],
            send_sem=block_sem.at[batch],
            recv_sem=blocks_sem.at[batch],
            device_id=peers[0],
            device_id_type=pl.DeviceIdType.MESH,
        )

    batches = devices // BATCH

    for batch in range(batches // 2):
        exchange_blocks(batch)
    own_copy.wait()

    own_goal = pltpu.make_async_copy(goal_ref.at[path], goals_ref.at[path], goals_sem.at[0])
    own_goal.start()
    goal_copies = []
    for step, other in enumerate(peers, 1):
        copy = pltpu.make_async_remote_copy(
            src_ref=goal_ref.at[other[0]],
            dst_ref=goals_ref.at[path],
            send_sem=goal_sem.at[step],
            recv_sem=goals_sem.at[step],
            device_id=other,
            device_id_type=pl.DeviceIdType.MESH,
        )
        copy.start()
        goal_copies.append(copy)

    second = {part: [] for part in range(len(PARTS))}

    def send_both(at, axis, columns):
        return [send(at, device(shifted(axis, step), core), full, columns) for step in (1, -1)]

    for part, (a, b, c, begin, end) in enumerate(PARTS):
        second[part].append(send_both(me, b, pl.ds(begin, end - begin)))
    halves = {}
    for index, step in ((0, 1), (1, -1)):
        for part, (a, b, c, begin, end) in enumerate(PARTS):
            columns = pl.ds(begin, end - begin)
            origin = shifted(a, -step)
            arrived(first[part][index], origin, full, columns)
            lines = low if index == 0 else high
            halves[part, index] = send(origin, device(shifted(a, step), core), lines, columns)
            second[part].append(send_both(origin, b, columns))
    for part, (a, b, c, begin, end) in enumerate(PARTS):
        columns = pl.ds(begin, end - begin)
        origin = shifted(a, 2)
        arrived(halves[part, 0], origin, low, columns)
        arrived(halves[part, 1], origin, high, columns)
        second[part].append(send_both(origin, b, columns))

    load_speed = pltpu.make_async_copy(speed_ref, rows_in, side_sem.at[0])
    load_speed.start()

    for batch in range(batches // 2, batches):
        exchange_blocks(batch)

    third = {part: [] for part in range(len(PARTS))}
    for part, (a, b, c, begin, end) in enumerate(PARTS):
        columns = pl.ds(begin, end - begin)
        line = {**me, a: whole}
        third[part].append(send_both(line, c, columns))
        share(line, columns)

    def origins(a):
        return [me[a], (me[a] + 3) % RING, (me[a] + 1) % RING, (me[a] + 2) % RING]

    for index, step in ((0, 1), (1, -1)):
        lines = low if index == 0 else high
        for part, (a, b, c, begin, end) in enumerate(PARTS):
            columns = pl.ds(begin, end - begin)
            far = shifted(b, -step)
            for unit, place in enumerate(origins(a)):
                origin = {**far, a: place}
                arrived(second[part][unit][index], origin, full, columns)
                halves[part, index, unit] = send(origin, device(shifted(b, step), core), lines, columns)
            line = {**far, a: whole}
            third[part].append(send_both(line, c, columns))
            share(line, columns)
    for part, (a, b, c, begin, end) in enumerate(PARTS):
        columns = pl.ds(begin, end - begin)
        far = shifted(b, 2)
        for unit, place in enumerate(origins(a)):
            origin = {**far, a: place}
            arrived(halves[part, 0, unit], origin, low, columns)
            arrived(halves[part, 1, unit], origin, high, columns)
        line = {**far, a: whole}
        third[part].append(send_both(line, c, columns))
        share(line, columns)

    for unit in range(RING):
        if unit == 1:
            load_speed.wait()
            turn_out(rows_in, turned, shards, paths)
            store_speed = pltpu.make_async_copy(turned, turned_ref, side_sem.at[0])
            store_speed.start()
        if unit == 3:
            own_block.wait()
            for batch in range(batches):
                exchanged(batch).wait_recv()
            turn_in(blocks_in, swap, columns_of)
            store_table = pltpu.make_async_copy(columns_of, table_ref, side_sem.at[1])
            store_table.start()
        for index, step in ((0, 1), (1, -1)):
            lines = low if index == 0 else high
            for part, (a, b, c, begin, end) in enumerate(PARTS):
                columns = pl.ds(begin, end - begin)
                far = {**shifted(c, -step), a: whole, b: origins(b)[unit]}
                arrived(third[part][unit][index], far, full, columns)
                halves[part, "last", index, unit] = send(far, device(shifted(c, step), core), lines, columns)
                share(far, columns)
    for unit in range(RING):
        for part, (a, b, c, begin, end) in enumerate(PARTS):
            columns = pl.ds(begin, end - begin)
            far = {**shifted(c, 2), a: whole, b: origins(b)[unit]}
            arrived(halves[part, "last", 0, unit], far, low, columns)
            arrived(halves[part, "last", 1, unit], far, high, columns)
            share(far, columns)
    for number, at, columns in sibling_arrivals:
        arrived(number, at, full, columns, 1 - core)
    for batch in range(batches):
        exchanged(batch).wait_send()
    store_speed.wait()
    store_table.wait()
    own_goal.wait()
    for step, copy in enumerate(goal_copies, 1):
        copy.wait_send()
        block = goals_ref.at[(path + paths - step) % paths]
        pltpu.make_async_remote_copy(
            src_ref=block,
            dst_ref=block,
            send_sem=goal_sem.at[step],
            recv_sem=goals_sem.at[step],
            device_id=peers[0],
            device_id_type=pl.DeviceIdType.MESH,
        ).wait_recv()
    for copy in sends:
        copy.wait_send()


COPIES = 156
BATCH = 16


def gather_tokens(own, goal, table, speed):
    rows, width = own.shape
    modules, rows_own, _ = table.shape
    paths, shards = lax.axis_size("path"), lax.axis_size("mp")
    groups, cols = modules * rows_own // 128, width // (paths * shards)
    anywhere = pl.BlockSpec(memory_space=pl.ANY)
    blocks = (paths * shards, groups, cols, 128)
    out, goals, table, speed = pl.pallas_call(
        gather_tokens_kernel,
        in_specs=[anywhere] * 4,
        out_specs=[anywhere] * 4,
        out_shape=[
            jax.ShapeDtypeStruct((paths // RING, RING, shards // 2, 2, rows, width), own.dtype),
            jax.ShapeDtypeStruct(goal.shape, goal.dtype),
            jax.ShapeDtypeStruct((modules, cols, width), table.dtype),
            jax.ShapeDtypeStruct(blocks, speed.dtype),
        ],
        scratch_shapes=[
            pltpu.VMEM((groups, 128, width), table.dtype),
            pltpu.VMEM(blocks, table.dtype),
            pltpu.VMEM(blocks, table.dtype),
            pltpu.VMEM(blocks, table.dtype),
            pltpu.VMEM((modules, cols, width), table.dtype),
            pltpu.VMEM((512, 512), jnp.bfloat16),
            pltpu.SemaphoreType.DMA,
            pltpu.SemaphoreType.DMA((COPIES,)),
            pltpu.SemaphoreType.DMA((COPIES,)),
            pltpu.SemaphoreType.DMA((paths,)),
            pltpu.SemaphoreType.DMA((paths,)),
            pltpu.SemaphoreType.DMA((paths * shards // BATCH,)),
            pltpu.SemaphoreType.DMA((paths * shards // BATCH,)),
            pltpu.SemaphoreType.DMA((2,)),
        ],
        compiler_params=pltpu.CompilerParams(
            vmem_limit_bytes=VMEM_LIMIT, collective_id=0, has_side_effects=True
        ),
        cost_estimate=pl.CostEstimate(
            flops=0, bytes_accessed=4 * paths * shards * rows * width, transcendentals=0
        ),
        name="gather_tokens",
    )(own, goal, table.reshape(groups, 128, width), speed.reshape(groups, 128, width))
    return out.reshape(paths * shards * rows, width), goals, table, speed


def unspread_kernel(blocks_ref, out_ref):
    shards, groups = blocks_ref.shape[1:3]
    for i in range(shards):
        for g in range(groups):
            turned = blocks_ref[:, i, g].reshape(-1, 128).T
            out_ref[g, :, i * turned.shape[1] : (i + 1) * turned.shape[1]] = turned


def unspread(blocks, modules, rows):
    paths, shards, groups, cols, _ = blocks.shape
    wide = paths * cols
    out = pl.pallas_call(
        unspread_kernel,
        grid=(shards // 2,),
        in_specs=[pl.BlockSpec((paths, 2, groups, cols, 128), lambda i: (0, i, 0, 0, 0))],
        out_specs=pl.BlockSpec((groups, 128, 2 * wide), lambda i: (0, 0, i)),
        out_shape=jax.ShapeDtypeStruct((groups, 128, wide * shards), blocks.dtype),
        compiler_params=pltpu.CompilerParams(vmem_limit_bytes=VMEM_LIMIT),
        name="unspread",
    )(blocks)
    return out.reshape(modules, rows, wide * shards)


def swap_matrix():
    index = jnp.arange(512)
    source, module, row = index // 128, (index // 32) % 4, index % 32
    return (index[:, None] == (module * 128 + source * 32 + row)[None, :]).astype(jnp.bfloat16)


CHUNK = 8


def outer_step(counts_ref, sums_ref, table_ref, speed_ref, swap_ref, updated_ref, out_ref, group):
    quads, cols = out_ref.shape[0] // 4, out_ref.shape[2]
    counts = [counts_ref[4 * group + q] for q in range(4)]
    for begin in range(0, quads, CHUNK):
        blocks = speed_ref[4 * begin : 4 * (begin + CHUNK), group].reshape(CHUNK, 4, cols, 128)
        line = jnp.concatenate([blocks[:, s].reshape(CHUNK * cols, 128) for s in range(4)], axis=1)
        speed = jnp.dot(line, swap_ref[...], preferred_element_type=jnp.float32).reshape(CHUNK, cols, 512)
        lines = []
        for k in range(CHUNK):
            moments = []
            for q in range(4):
                columns = slice((begin + k) * 128, (begin + k + 1) * 128)
                average = sums_ref[4 * group + q, :, columns] / counts[q]
                moment = outer_momentum * speed[k, :, q * 128 : (q + 1) * 128] + average
                begun = table_ref[4 * group + q, :, columns].astype(jnp.float32)
                updated_ref[4 * group + q, :, columns] = (
                    begun - outer_rate * (average + outer_momentum * moment)
                ).astype(jnp.bfloat16)
                moments.append(moment.astype(jnp.bfloat16))
            lines.append(jnp.concatenate(moments, axis=1))
        line = jnp.concatenate(lines, axis=0)
        turned = jnp.dot(line, swap_ref[...], preferred_element_type=jnp.float32).astype(jnp.bfloat16)
        turned = turned.reshape(CHUNK, cols, 512)
        for k in range(CHUNK):
            for s in range(4):
                out_ref[4 * (begin + k) + s, group] = turned[k, :, s * 128 : (s + 1) * 128]


def pieces(value):
    high = value.astype(jnp.bfloat16)
    rest = value - high.astype(jnp.float32)
    middle = rest.astype(jnp.bfloat16)
    low = (rest - middle.astype(jnp.float32)).astype(jnp.bfloat16)
    return jnp.concatenate([high, middle, low], axis=0)


def slopes(weights, normed, goal):
    cols = goal.shape[0]
    both = jnp.dot(weights, normed, preferred_element_type=jnp.float32)
    gate_act, up_act = both[:cols], both[cols:]
    sigma = jax.nn.sigmoid(gate_act)
    swish = gate_act * sigma
    error = (swish * up_act - goal) / TOK_PATH
    d_gate = error * up_act * sigma * (1.0 + gate_act * (1.0 - sigma))
    d_up = error * swish
    return pieces(jnp.concatenate([d_gate, d_up], axis=0))


TILE = 512


def inner_kernel(lists_ref, normed_ref, goal_ref, table_ref, sums_ref, start, current, first_grad, master, slope, turned):
    path = pl.program_id(0)
    gate, up = lists_ref[2 * path], lists_ref[2 * path + 1]
    cols = goal_ref.shape[1]
    width = normed_ref.shape[1]

    @pl.when(path == 0)
    def _():
        sums_ref[...] = jnp.zeros_like(sums_ref)

    start[:cols] = table_ref[gate]
    start[cols:] = table_ref[up]
    goal = goal_ref[0].astype(jnp.float32)
    for j in range(width // 512):
        turned[j * 512 : (j + 1) * 512, :] = normed_ref[:, j * 512 : (j + 1) * 512].T
    slope[...] = slopes(start[...], turned[...], goal)

    def product(columns):
        parts = jnp.dot(slope[...], normed_ref[:, columns], preferred_element_type=jnp.float32)
        return parts[: 2 * cols] + (parts[2 * cols : 4 * cols] + parts[4 * cols :])

    def sweep(update):
        tiles = [slice(j * TILE, (j + 1) * TILE) for j in range(width // TILE)]
        grad = product(tiles[0])
        for this, following in zip(tiles, tiles[1:] + [None]):
            later = product(following) if following is not None else None
            update(this, grad)
            grad = later

    def first_step(columns, grad):
        first_grad[:, columns] = grad
        begin = start[:, columns].astype(jnp.float32)
        after = begin - inner_rate * (grad / (jnp.abs(grad) + adam_epsilon) + weight_decay * begin)
        master[:, columns] = after
        current[:, columns] = after.astype(jnp.bfloat16)

    def second_step(columns, grad):
        before = first_grad[:, columns]
        begin = start[:, columns].astype(jnp.float32)
        after = master[:, columns]
        first = (beta_first * (1.0 - beta_first) / (1.0 - beta_first**2)) * before + (
            (1.0 - beta_first) / (1.0 - beta_first**2)
        ) * grad
        second = (beta_second * (1.0 - beta_second) / (1.0 - beta_second**2)) * before * before + (
            (1.0 - beta_second) / (1.0 - beta_second**2)
        ) * grad * grad
        after = after - inner_rate * (
            first / (jnp.sqrt(second) + adam_epsilon) + weight_decay * after
        )
        delta = (begin - after).astype(jnp.bfloat16).astype(jnp.float32)
        sums_ref[gate, :, columns] += delta[:cols]
        sums_ref[up, :, columns] += delta[cols:]

    sweep(first_step)
    slope[...] = slopes(current[...], turned[...], goal)
    sweep(second_step)


def inner_steps(lists, normed, goals, table):
    modules, cols, width = table.shape
    paths = goals.shape[0]
    tokens = normed.shape[0]
    return pl.pallas_call(
        inner_kernel,
        grid_spec=pltpu.PrefetchScalarGridSpec(
            num_scalar_prefetch=1,
            grid=(paths,),
            in_specs=[
                pl.BlockSpec((TOK_PATH, width), lambda p, s: (p, 0)),
                pl.BlockSpec((1, cols, TOK_PATH), lambda p, s: (p, 0, 0)),
                pl.BlockSpec((modules, cols, width), lambda p, s: (0, 0, 0)),
            ],
            out_specs=pl.BlockSpec((modules, cols, width), lambda p, s: (0, 0, 0)),
            scratch_shapes=[
                pltpu.VMEM((2 * cols, width), jnp.bfloat16),
                pltpu.VMEM((2 * cols, width), jnp.bfloat16),
                pltpu.VMEM((2 * cols, width), jnp.float32),
                pltpu.VMEM((2 * cols, width), jnp.float32),
                pltpu.VMEM((6 * cols, TOK_PATH), jnp.bfloat16),
                pltpu.VMEM((width, TOK_PATH), jnp.bfloat16),
            ],
        ),
        out_shape=jax.ShapeDtypeStruct((modules, cols, width), jnp.float32),
        compiler_params=pltpu.CompilerParams(vmem_limit_bytes=VMEM_LIMIT),
        cost_estimate=pl.CostEstimate(
            flops=32 * tokens * width * cols, bytes_accessed=2 * tokens * width, transcendentals=0
        ),
        name="inner_steps",
    )(lists, normed, goals, table)


def finish_kernel(
    lists_ref, counts_ref, normed_ref, sums_ref, table_ref, speed_ref, moments_ref, out_ref,
    sums, begun, speed, updated, blocks_out, blocks_in, swap, weights, outgoing, arrived,
    send_sem, recv_sem, block_sem, blocks_sem, sums_sem, side_sem,
):
    target = pl.program_id(0)
    path, shard = lax.axis_index("path"), lax.axis_index("mp")
    paths, cols, tokens = arrived.shape

    def remote(block, at, number, other):
        return pltpu.make_async_remote_copy(
            src_ref=outgoing.at[block],
            dst_ref=arrived.at[at],
            send_sem=send_sem.at[block],
            recv_sem=recv_sem.at[number],
            device_id=(other, shard),
            device_id_type=pl.DeviceIdType.MESH,
        )

    devices, groups = blocks_out.shape[:2]
    shards = devices // paths
    mine = path * shards + shard
    batches = devices // BATCH

    def exchanged(batch):
        amount = BATCH - 1 if batch == 0 else BATCH
        return pltpu.make_async_remote_copy(
            src_ref=blocks_out.at[pl.ds(0, amount)],
            dst_ref=blocks_in.at[pl.ds(0, amount)],
            send_sem=block_sem.at[batch],
            recv_sem=blocks_sem.at[batch],
            device_id=((path + 1) % paths, shard),
            device_id_type=pl.DeviceIdType.MESH,
        )

    def own_block():
        return pltpu.make_async_copy(blocks_out.at[mine], blocks_in.at[mine], side_sem.at[0])

    @pl.when(target == 0)
    def _():
        load_table = pltpu.make_async_copy(table_ref, begun, side_sem.at[0])
        load_speed = pltpu.make_async_copy(speed_ref, speed, side_sem.at[1])
        load_speed.start()
        load_table.start()
        for g in range(groups):
            part = pl.ds(4 * g, 4)
            pltpu.make_async_copy(sums_ref.at[part], sums.at[part], sums_sem.at[g]).start()
        barrier = pltpu.get_barrier_semaphore()

        @pl.loop(1, devices)
        def _(step):
            other = (mine + 37 * step) % devices
            pl.semaphore_signal(
                barrier, inc=1, device_id=(other // shards, other % shards), device_id_type=pl.DeviceIdType.MESH
            )

        swap[...] = swap_values()
        load_speed.wait()
        load_table.wait()

        @pl.loop(0, groups)
        def _(group):
            part = pl.ds(4 * group, 4)
            pltpu.make_async_copy(sums_ref.at[part], sums.at[part], sums_sem.at[group]).wait()
            outer_step(counts_ref, sums, begun, speed, swap, updated, blocks_out, group)

        own_block().start()
        pl.semaphore_wait(barrier, devices - 1)
        for batch in range(batches):

            @pl.loop(max(batch * BATCH, 1), (batch + 1) * BATCH)
            def _(step):
                other = (mine + 37 * step) % devices
                pltpu.make_async_remote_copy(
                    src_ref=blocks_out.at[other],
                    dst_ref=blocks_in.at[mine],
                    send_sem=block_sem.at[batch],
                    recv_sem=blocks_sem.at[batch],
                    device_id=(other // shards, other % shards),
                    device_id_type=pl.DeviceIdType.MESH,
                ).start()

    weights[:cols] = updated[lists_ref[2 * target]]
    weights[cols:] = updated[lists_ref[2 * target + 1]]
    both = lax.dot_general(weights[...], normed_ref[...], NT, preferred_element_type=jnp.float32)
    gate_act = both[:cols]
    result = (gate_act * jax.nn.sigmoid(gate_act) * both[cols:]).astype(jnp.bfloat16)

    @pl.when(target == path)
    def _():
        arrived[path] = result

    @pl.when(target != path)
    def _():
        outgoing[target] = result
        remote(target, path, path, target).start()

    @pl.when(target == paths - 1)
    def _():
        for step in range(1, paths):
            other = (path + step) % paths
            remote(other, other, other, other).wait()
        out_ref[...] = arrived[...].reshape(paths * cols, tokens).T
        own_block().wait()
        for batch in range(batches):
            exchanged(batch).wait()
        store = pltpu.make_async_copy(blocks_in, moments_ref, side_sem.at[0])
        store.start()
        store.wait()


def finish(lists, counts, normed, sums, table, speed):
    modules, cols, width = table.shape
    tokens = normed.shape[0]
    paths = tokens // TOK_PATH
    scalars, anywhere = pl.BlockSpec(memory_space=pltpu.SMEM), pl.BlockSpec(memory_space=pl.ANY)
    return pl.pallas_call(
        finish_kernel,
        grid=(paths,),
        in_specs=[
            scalars,
            scalars,
            pl.BlockSpec((TOK_PATH, width), lambda p: (p, 0)),
            anywhere,
            anywhere,
            anywhere,
        ],
        out_specs=[anywhere, pl.BlockSpec((TOK_PATH, paths * cols), lambda p: (0, 0))],
        scratch_shapes=[
            pltpu.VMEM(sums.shape, sums.dtype),
            pltpu.VMEM(table.shape, table.dtype),
            pltpu.VMEM(speed.shape, speed.dtype),
            pltpu.VMEM(table.shape, table.dtype),
            pltpu.VMEM(speed.shape, speed.dtype),
            pltpu.VMEM(speed.shape, speed.dtype),
            pltpu.VMEM((512, 512), jnp.bfloat16),
            pltpu.VMEM((2 * cols, width), jnp.bfloat16),
            pltpu.VMEM((paths, cols, TOK_PATH), jnp.bfloat16),
            pltpu.VMEM((paths, cols, TOK_PATH), jnp.bfloat16),
            pltpu.SemaphoreType.DMA((paths,)),
            pltpu.SemaphoreType.DMA((paths,)),
            pltpu.SemaphoreType.DMA((speed.shape[0] // BATCH,)),
            pltpu.SemaphoreType.DMA((speed.shape[0] // BATCH,)),
            pltpu.SemaphoreType.DMA((speed.shape[1],)),
            pltpu.SemaphoreType.DMA((2,)),
        ],
        out_shape=[
            jax.ShapeDtypeStruct(speed.shape, speed.dtype),
            jax.ShapeDtypeStruct((TOK_PATH, paths * cols), jnp.bfloat16),
        ],
        compiler_params=pltpu.CompilerParams(
            vmem_limit_bytes=VMEM_LIMIT, collective_id=1, has_side_effects=True
        ),
        cost_estimate=pl.CostEstimate(
            flops=4 * tokens * width * cols, bytes_accessed=2 * tokens * width, transcendentals=0
        ),
        name="finish",
    )(lists, counts, normed, sums, table, speed)


def exchange(blocks, axes):
    return lax.all_to_all(blocks, axes, split_axis=0, concat_axis=0, tiled=True)


def local(features, targets, module_table, momentum, path_lists):
    paths = lax.axis_size("path")
    shards = lax.axis_size("mp")
    modules, rows_own, width = module_table.shape
    cols = width // (paths * shards)
    lists = path_lists.reshape(-1)
    both = ("path", "mp")

    def sent(blocks):
        return exchange(blocks.reshape((paths * shards,) + blocks.shape[-3:]), both)

    own, goal = normalize(features), targets.T.reshape(paths, cols, TOK_PATH)
    normed, goals, table, speed = gather_tokens(own, goal, module_table, momentum)
    speed = sent(speed)
    select = lists[None, :] == jnp.arange(modules, dtype=jnp.int32)[:, None]
    counts = jnp.sum(select.astype(jnp.float32), axis=1)
    sums = inner_steps(lists, normed, goals, table)
    blocks, evaluated = finish(lists, counts, normed, sums, table, speed)
    momentum_out = unspread(blocks.reshape((paths, shards) + blocks.shape[1:]), modules, rows_own)
    return (momentum_out, evaluated)


def solution(mesh):
    return jax.shard_map(
        local,
        mesh=mesh,
        in_specs=(
            P(("path", "mp"), None),
            P("path", "mp"),
            P(None, ("path", "mp"), None),
            P(None, ("path", "mp"), None),
            P(),
        ),
        out_specs=(P(None, ("path", "mp"), None), P("path", "mp")),
        check_vma=False,
    )
```
